128 devices in a mesh: lat: 8 (over x_hi, y), lon: 16 (over z, x_lo, core).
Axes of the slice: x: 4 (x_hi: 2, x_lo: 2; x = x_hi * 2 + x_lo), y: 4, z: 4, core: 2. Of those that a mesh axis runs over, the one named last changes fastest.
Arguments:
- tokens: bfloat16 [1, 96, 384, 512], P(None, 'lat', 'lon'), may hold values from -6 to 6
- cot_fine: bfloat16 [1, 96, 384, 512], P(None, 'lat', 'lon'), may hold values from -6 to 6
- cot_coarse: bfloat16 [1, 48, 192, 1024], P(None, 'lat', 'lon'), may hold values from -6 to 6
- mask_ids: int32 [1, 96, 384], P(None, 'lat', 'lon'), may hold values from 0 to 3
- pad_flags: int32 [1, 96, 384], P(None, 'lat', 'lon'), may hold values 0 or 1
- w_qkv_fine: bfloat16 [512, 1536], replicated, may hold values from -6 to 6
- w_out_fine: bfloat16 [512, 512], replicated, may hold values from -0.25 to 0.25
- w_merge: bfloat16 [2048, 1024], replicated, may hold values from -0.125 to 0.125
- w_qkv_coarse: bfloat16 [1024, 3072], replicated, may hold values from -6 to 6
- w_out_coarse: bfloat16 [1024, 1024], replicated, may hold values from -0.1875 to 0.1875
Outputs:
- grad_tokens: bfloat16 [1, 96, 384, 512], P(None, 'lat', 'lon')
- grad_flat: float32 [4194304], P(('lat', 'lon'))
The draws below stay inside these ranges and needn't reach their ends.
All inputs are finite; a program needn't handle non-finite values. No bound on the sum of `pad_flags` on one device may be relied on, other than what follows from the above.
Results may differ from the reference program's by a relative error of at most 0.02.
Values may be sent and summed in bfloat16 or wider, within the bound.
A program may use at most 192 MiB of HBM per device.

```python
import jax
import jax.numpy as jnp
from jax import lax

WIDTH_FINE = 512
WIDTH_COARSE = 1024
HEADS_FINE = 8
HEADS_COARSE = 16
LEVELS = 1
WIN_LAT = 6
WIN_LON = 12
LAT = 96
LON = 384


def drawn_qkv(key, channels):
    base_draw = jax.random.normal(key, (channels, 3 * channels), jnp.float32)
    return jnp.clip(base_draw, -4.0, 4.0) * channels ** (-0.5)


def draw_w_qkv_fine(key, part):
    key = jax.random.fold_in(key, 11)
    return drawn_qkv(key, WIDTH_FINE).astype(jnp.bfloat16)


def draw_w_qkv_coarse(key, part):
    key = jax.random.fold_in(key, 13)
    return drawn_qkv(key, WIDTH_COARSE).astype(jnp.bfloat16)


def plant(values, rng, least, top_value):
    shape = values.shape
    place = [jax.random.randint(jax.random.fold_in(rng, axis), (), 0, shape[axis]) for axis in range(len(shape))]
    values = values.at[tuple(place)].set(least)
    longest = shape.index(max(shape))
    place[longest] = (place[longest] + 1) % shape[longest]
    return values.at[tuple(place)].set(top_value)


def steps_of(rng, shape, cuts, low, top_value):
    factor_of, own = 1.0, jax.random.fold_in(rng, 6)
    for position, parts in cuts:
        heights = jnp.exp(jax.random.uniform(jax.random.fold_in(own, position), (parts,), jnp.float32, low / len(cuts), top_value / len(cuts)))
        factor_of = factor_of * jnp.repeat(heights, shape[position] // parts).reshape([-1 if axis == position else 1 for axis in range(len(shape))])
    return factor_of


def gaussian(stream_key, shape, width, most, cuts=(), kind=jnp.bfloat16):
    values = jax.random.normal(stream_key, shape, jnp.float32) * width
    if len(cuts) > 0:
        values = steps_of(stream_key, shape, cuts, -0.22, 0.18) * values
    return jnp.clip(values, min=-most, max=most).astype(kind)


def setup_inputs(seed: int = 0) -> dict:
    keys = jax.random.split(jax.random.key(seed), 11)
    return {
        "tokens": gaussian(keys[0], (LEVELS, LAT, LON, WIDTH_FINE), 1.0, 6.0, ((1, 8), (2, 16))),
        "cot_fine": gaussian(keys[1], (LEVELS, LAT, LON, WIDTH_FINE), 1.0, 6.0, ((1, 8), (2, 16))),
        "cot_coarse": gaussian(keys[2], (LEVELS, LAT // 2, LON // 2, WIDTH_COARSE), 1.0, 6.0, ((1, 8), (2, 16))),
        "mask_ids": plant(jax.random.randint(keys[3], (LEVELS, LAT, LON), 0, 4), jax.random.fold_in(keys[3], 1), 0, 3).astype(jnp.int32),
        "pad_flags": plant((jax.random.randint(keys[4], (LEVELS, LAT, LON), 0, 8) < 7).astype(jnp.int32), jax.random.fold_in(keys[4], 1), 0, 1),
        "w_qkv_fine": draw_w_qkv_fine(jax.random.fold_in(keys[10], 71), 0),
        "w_out_fine": gaussian(keys[6], (WIDTH_FINE, WIDTH_FINE), WIDTH_FINE ** -0.5, 0.25),
        "w_merge": gaussian(keys[7], (4 * WIDTH_FINE, WIDTH_COARSE), (4 * WIDTH_FINE) ** -0.5, 0.125),
        "w_qkv_coarse": draw_w_qkv_coarse(jax.random.fold_in(keys[10], 71), 0),
        "w_out_coarse": gaussian(keys[9], (WIDTH_COARSE, WIDTH_COARSE), WIDTH_COARSE ** -0.5, 0.1875),
    }


HIGHEST = lax.Precision.HIGHEST

def norm_rows(values):
    average = lax.optimization_barrier(jnp.mean(values, axis=-1, keepdims=True))
    centred = values - average
    spread = lax.optimization_barrier(jnp.mean(centred * centred, axis=-1, keepdims=True))
    return centred * lax.rsqrt(spread + 1e-05)

def norm_back(values, grad_out):
    return jax.vjp(norm_rows, values)[1](grad_out)[0]

def matmul(left_side, right_side):
    return jnp.dot(left_side, right_side, preferred_element_type=jnp.float32)

def matmul_tn(left_side, right_side):
    return lax.dot_general(left_side, right_side, (((0,), (0,)), ((), ())), preferred_element_type=jnp.float32)

def matmul_nt(left_side, right_side):
    return lax.dot_general(left_side, right_side, (((1,), (1,)), ((), ())), preferred_element_type=jnp.float32)

def attend(packed, labels, head_count):
    count, window_len, triple = packed.shape
    feat_width = triple // 3
    head_size = feat_width // head_count
    queries = packed[..., :feat_width].reshape(count, window_len, head_count, head_size)
    key_rows = packed[..., feat_width:2 * feat_width].reshape(count, window_len, head_count, head_size)
    values = packed[..., 2 * feat_width:].reshape(count, window_len, head_count, head_size)
    scores = jnp.einsum('nqhd,nkhd->nhqk', queries, key_rows, precision=HIGHEST) * head_size ** (-0.5)
    allowed = (labels[:, :, None] == labels[:, None, :])[:, None]
    scores = jnp.where(allowed, scores, -1e+30)
    row_peak = lax.stop_gradient(lax.optimization_barrier(jnp.max(scores, axis=-1, keepdims=True)))
    weights = jnp.exp(scores - row_peak)
    shares = weights / lax.optimization_barrier(jnp.sum(weights, axis=-1, keepdims=True))
    result = jnp.einsum('nhqk,nkhd->nqhd', shares, values, precision=HIGHEST)
    return result.reshape(count, window_len, feat_width)

def to_windows(grid_in):
    level_count, row_count, col_count, channels = grid_in.shape
    pieces = grid_in.reshape(level_count, row_count // WIN_LAT, WIN_LAT, col_count // WIN_LON, WIN_LON, channels)
    return pieces.transpose(1, 3, 0, 2, 4, 5).reshape(row_count // WIN_LAT, col_count // WIN_LON, level_count * WIN_LAT * WIN_LON, channels)

def from_windows(blocks, level_count):
    lat_blocks, lon_blocks, window_len, channels = blocks.shape
    pieces = blocks.reshape(lat_blocks, lon_blocks, level_count, WIN_LAT, WIN_LON, channels)
    return pieces.transpose(2, 0, 3, 1, 4, 5).reshape(level_count, lat_blocks * WIN_LAT, lon_blocks * WIN_LON, channels)

def window_attention(packed, labels, head_count):
    half_lat = WIN_LAT // 2
    half_lon = WIN_LON // 2
    rolled = jnp.roll(packed, (-half_lat, -half_lon), (1, 2))
    rolled_ids = jnp.roll(labels, (-half_lat, -half_lon), (1, 2))
    blocks = to_windows(rolled)
    id_blocks = to_windows(rolled_ids[..., None])[..., 0]
    checked = jax.checkpoint(lambda packed_in, labels_in: attend(packed_in, labels_in, head_count))
    mapped = lax.map(lambda pair_in: checked(pair_in[0], pair_in[1]), (blocks, id_blocks))
    restored = from_windows(mapped, packed.shape[0])
    return jnp.roll(restored, (half_lat, half_lon), (1, 2))

def merge_tokens(grid_in):
    level_count, row_count, col_count, channels = grid_in.shape
    pieces = grid_in.reshape(level_count, row_count // 2, 2, col_count // 2, 2, channels)
    return pieces.transpose(0, 1, 3, 2, 4, 5).reshape(level_count, row_count // 2, col_count // 2, 4 * channels)

def split_tokens(grid_in, channels):
    level_count, row_count, col_count, wide = grid_in.shape
    pieces = grid_in.reshape(level_count, row_count, col_count, 2, 2, channels)
    return pieces.transpose(0, 1, 3, 2, 4, 5).reshape(level_count, 2 * row_count, 2 * col_count, channels)

def reference(tokens, cot_fine, cot_coarse, mask_ids, pad_flags, w_qkv_fine, w_out_fine, w_merge, w_qkv_coarse, w_out_coarse):
    level_count = tokens.shape[0]
    fine_in = tokens.astype(jnp.float32)
    normed_fine = norm_rows(fine_in).astype(jnp.bfloat16).reshape(-1, WIDTH_FINE)
    packed_fine = matmul(normed_fine, w_qkv_fine).reshape(level_count, LAT, LON, 3 * WIDTH_FINE)
    attn_fine, back_fine = jax.vjp(lambda packed: window_attention(packed, mask_ids, HEADS_FINE), packed_fine)
    mixed_fine = attn_fine.astype(jnp.bfloat16).reshape(-1, WIDTH_FINE)
    fine_out = (fine_in + matmul(mixed_fine, w_out_fine).reshape(fine_in.shape)).astype(jnp.bfloat16)
    merged = merge_tokens(fine_out).astype(jnp.float32).reshape(-1, 4 * WIDTH_FINE)
    normed_merge = norm_rows(merged).astype(jnp.bfloat16)
    coarse_in = matmul(normed_merge, w_merge).astype(jnp.bfloat16)
    coarse_wide = coarse_in.astype(jnp.float32)
    normed_coarse = norm_rows(coarse_wide).astype(jnp.bfloat16)
    packed_coarse = matmul(normed_coarse, w_qkv_coarse).reshape(level_count, LAT // 2, LON // 2, 3 * WIDTH_COARSE)
    coarse_ids = mask_ids[:, ::2, ::2]
    attn_coarse, back_coarse = jax.vjp(lambda packed: window_attention(packed, coarse_ids, HEADS_COARSE), packed_coarse)
    mixed_coarse = attn_coarse.astype(jnp.bfloat16).reshape(-1, WIDTH_COARSE)
    grad_top = cot_coarse.reshape(-1, WIDTH_COARSE)
    grad_out_coarse = matmul_tn(mixed_coarse, grad_top)
    grad_mixed_coarse = matmul_nt(grad_top, w_out_coarse).astype(jnp.bfloat16)
    grad_packed_coarse = back_coarse(grad_mixed_coarse.astype(jnp.float32).reshape(attn_coarse.shape))[0]
    grad_packed_coarse = grad_packed_coarse.reshape(-1, 3 * WIDTH_COARSE).astype(jnp.bfloat16)
    grad_normed_coarse = matmul_nt(grad_packed_coarse, w_qkv_coarse)
    grad_coarse = (grad_top.astype(jnp.float32) + norm_back(coarse_wide, grad_normed_coarse)).astype(jnp.bfloat16)
    grad_merge = matmul_tn(normed_merge, grad_coarse)
    grad_normed_merge = matmul_nt(grad_coarse, w_merge)
    grad_merged = norm_back(merged, grad_normed_merge).reshape(level_count, LAT // 2, LON // 2, 4 * WIDTH_FINE)
    flag_rows = pad_flags[..., None].astype(jnp.float32)
    grad_fine_out = flag_rows * cot_fine.astype(jnp.float32) + split_tokens(grad_merged, WIDTH_FINE)
    grad_fine_low = grad_fine_out.astype(jnp.bfloat16).reshape(-1, WIDTH_FINE)
    grad_out_fine = matmul_tn(mixed_fine, grad_fine_low)
    grad_mixed_fine = matmul_nt(grad_fine_low, w_out_fine).astype(jnp.bfloat16)
    grad_packed_fine = back_fine(grad_mixed_fine.astype(jnp.float32).reshape(attn_fine.shape))[0]
    grad_packed_fine = grad_packed_fine.reshape(-1, 3 * WIDTH_FINE).astype(jnp.bfloat16)
    grad_qkv_fine = matmul_tn(normed_fine, grad_packed_fine)
    grad_normed_fine = matmul_nt(grad_packed_fine, w_qkv_fine).reshape(fine_in.shape)
    grad_tokens = (grad_fine_out + norm_back(fine_in, grad_normed_fine)).astype(jnp.bfloat16)
    grad_flat = jnp.concatenate([grad_qkv_fine.reshape(-1), grad_out_fine.reshape(-1), grad_merge.reshape(-1), grad_out_coarse.reshape(-1)])
    return (grad_tokens, grad_flat)
```

```python
import functools
import types

import jax
import jax.numpy as jnp
import numpy as np
from jax import lax
from jax.experimental import pallas as pl
from jax.experimental.pallas import tpu as pltpu
from jax.sharding import PartitionSpec as P

WIN_LAT = 6
WIN_LON = 12
ROWS = 12
COLS = 24
CELLS = ROWS * COLS
WINDOW = WIN_LAT * WIN_LON
WIDE = 512
COARSE = 1024
HEAD = 64
PAIR = 2 * HEAD
AUX = 128
MESH = pl.DeviceIdType.MESH
F32 = jnp.float32
BF16 = jnp.bfloat16

KEPT = 176
PARTS = ((176, 64), (240, 64), (304, 32))
SLOTS = 336
KEPT_C = 32
PARTS_C = ((32, 32), (64, 32), (96, 32))
SLOTS_C = 128


def slot_of(a, b, half_lat, half_lon, cols, offsets):
    if a >= half_lat and b >= half_lon:
        return (a - half_lat) * (cols - half_lon) + b - half_lon
    if b >= half_lon:
        return offsets[0] + a * (cols - half_lon) + b - half_lon
    if a >= half_lat:
        return offsets[1] + (a - half_lat) * half_lon + b
    return offsets[2] + a * half_lon + b


(
    SEND_ROWS, TAKE_WINDOWS, SEND_WINDOWS, TAKE_MERGE,
    SEND_ROWS_T, TAKE_WINDOWS_T, SEND_WINDOWS_T, TAKE_MERGE_T,
    SEND_COARSE, TAKE_COARSE, SEND_IDS, ROW_OF, COL_OF,
) = range(13)


def index_maps():
    fine = [off for off, _ in PARTS]
    coarse = [off for off, _ in PARTS_C]
    table = np.full((SLOTS, AUX), -1, np.int32)
    for a in range(ROWS):
        for b in range(COLS):
            cell = a * COLS + b
            here = slot_of(a, b, 3, 6, COLS, fine)
            came = slot_of((a + 3) % ROWS, (b + 6) % COLS, 3, 6, COLS, fine)
            window = (a // 6 * 2 + b // 12) * WINDOW + a % 6 * 12 + b % 12
            quarter = (a % 2 * 2 + b % 2) * WINDOW + a // 2 * 12 + b // 2
            for name, row, source in (
                (SEND_ROWS, here, cell),
                (TAKE_WINDOWS, window, came),
                (SEND_WINDOWS, here, window),
                (TAKE_MERGE, quarter, came),
            ):
                table[row, name] = source
                table[source, name + SEND_ROWS_T] = row
            table[cell, ROW_OF] = a
            table[cell, COL_OF] = b
    for i in range(6):
        for j in range(12):
            here = slot_of(i, j, 3, 6, 12, coarse)
            came = slot_of((i + 3) % 6, (j + 6) % 12, 3, 6, 12, coarse)
            table[here, SEND_COARSE] = i * 12 + j
            table[i * 12 + j, TAKE_COARSE] = came
            table[here, SEND_IDS] = 2 * i * COLS + 2 * j
    return table


def dot(a, b):
    return jnp.dot(a, b, preferred_element_type=F32)


def dot_nt(a, b):
    return lax.dot_general(a, b, (((1,), (1,)), ((), ())), preferred_element_type=F32)


def dot_tn(a, b):
    return lax.dot_general(a, b, (((0,), (0,)), ((), ())), preferred_element_type=F32)


def norm_parts(parts):
    size = sum(p.shape[-1] for p in parts)
    average = sum(jnp.sum(p, axis=-1, keepdims=True) for p in parts) * (1.0 / size)
    centred = [p - average for p in parts]
    spread = sum(jnp.sum(c * c, axis=-1, keepdims=True) for c in centred) * (1.0 / size)
    scale = lax.rsqrt(spread + 1e-05)
    return [c * scale for c in centred], scale


def norm_parts_back(normed, scale, grads):
    size = sum(p.shape[-1] for p in normed)
    flat = sum(jnp.sum(g, axis=-1, keepdims=True) for g in grads) * (1.0 / size)
    along = sum(
        jnp.sum(g * n, axis=-1, keepdims=True) for g, n in zip(grads, normed)
    ) * (1.0 / size)
    return [scale * (g - flat - n * along) for g, n in zip(grads, normed)]


def first_lanes():
    return lax.broadcasted_iota(jnp.int32, (WINDOW, PAIR), 1) < HEAD


def stacked(x, low):
    return jnp.concatenate([jnp.where(low, x, 0.0), jnp.where(low, 0.0, x)], axis=0)


def split_bf16(x):
    high = x.astype(BF16)
    return high, (x - high.astype(F32)).astype(BF16)


def allowed_of(ids):
    pick = (lax.broadcasted_iota(jnp.int32, (8, AUX), 1) == 0).astype(BF16)
    along = dot_nt(pick, ids.astype(BF16))[0:1]
    same = ids[:, 0:1] == along
    return jnp.concatenate([same, same], axis=0)


def pair_forward(q, k, v, allowed, low):
    q_high, q_low = split_bf16(stacked(q, low))
    k_high, k_low = split_bf16(k)
    scores = dot_nt(q_high, k_high) + dot_nt(q_high, k_low) + dot_nt(q_low, k_high)
    scores = jnp.where(allowed, scores * HEAD**-0.5, -1e30)
    weights = jnp.exp(scores - jnp.max(scores, axis=-1, keepdims=True))
    shares = weights / jnp.sum(weights, axis=-1, keepdims=True)
    result = dot(shares.astype(BF16), v.astype(BF16))
    return shares, jnp.where(low, result[:WINDOW], result[WINDOW:])


def pair_backward(q, k, v, shares, grad, low):
    grad2 = stacked(grad, low).astype(BF16)
    q2 = stacked(q, low).astype(BF16)
    grad_shares = dot_nt(grad2, v.astype(BF16))
    delta = jnp.sum(grad_shares * shares, axis=-1, keepdims=True)
    grad_scores = (shares * (grad_shares - delta) * HEAD**-0.5).astype(BF16)
    grad_q = dot(grad_scores, k.astype(BF16))
    grad_q = jnp.where(low, grad_q[:WINDOW], grad_q[WINDOW:])
    return grad_q, dot_tn(grad_scores, q2), dot_tn(shares.astype(BF16), grad2)


def attend(packed, shares, attn, ids, windows, width):
    pairs = width // PAIR

    def window(w, carry):
        rows = pl.ds(pl.multiple_of(w * WINDOW, 8), WINDOW)
        low = first_lanes()
        allowed = allowed_of(ids[rows])
        for p in range(pairs):
            q, k, v = (
                packed[rows, t * width + p * PAIR : t * width + (p + 1) * PAIR]
                for t in range(3)
            )
            part, result = pair_forward(q, k, v, allowed, low)
            shares[w * pairs + p] = part
            attn[rows, p * PAIR : (p + 1) * PAIR] = result
        return carry

    lax.fori_loop(0, windows, window, 0)


def attend_back(packed, shares, grad, grad_packed, windows, width):
    pairs = width // PAIR

    def window(w, carry):
        rows = pl.ds(pl.multiple_of(w * WINDOW, 8), WINDOW)
        low = first_lanes()
        for p in range(pairs):
            q, k, v = (
                packed[rows, t * width + p * PAIR : t * width + (p + 1) * PAIR]
                for t in range(3)
            )
            grads = pair_backward(
                q, k, v, shares[w * pairs + p],
                grad[rows, p * PAIR : (p + 1) * PAIR], low,
            )
            for t in range(3):
                grad_packed[rows, t * width + p * PAIR : t * width + (p + 1) * PAIR] = grads[t]
        return carry

    lax.fori_loop(0, windows, window, 0)


SEGMENTS = dict(
    out_c=(6, 2, 32, 1024),
    merge=(2, 4, 32, 1024),
    fine=(0, 2, 64, 512),
)


class Summed:
    def __init__(self, r, name, place):
        self.first, self.lats, self.rows, self.cols = SEGMENTS[name]
        self.r, self.name, self.place = r, name, place
        self.final = r.final_fine if self.rows == 64 else r.final_coarse
        self.final_sem = r.final_recv_fine if self.rows == 64 else r.final_recv_coarse

    def ref(self, what):
        return getattr(self.r, what + "_" + self.name)

    def copy(self, src, dst, send_sem, recv_sem, lat, lon):
        return pltpu.make_async_remote_copy(
            src_ref=src, dst_ref=dst, send_sem=send_sem, recv_sem=recv_sem,
            device_id=(lat, lon), device_id_type=MESH,
        )

    def start_core(self):
        lat, z, x, core = self.place
        send, recv = self.ref("ssend"), self.ref("srecv")
        self.core_copy = self.copy(
            self.ref("part").at[:, 1 - core], self.ref("core"), send.at[0], recv.at[0],
            lat, z * 4 + x * 2 + 1 - core,
        )
        self.core_copy.start()

    def start_z(self):
        lat, z, x, core = self.place
        send, recv = self.ref("ssend"), self.ref("srecv")
        part, other, both = self.ref("part"), self.ref("core"), self.ref("both")
        self.core_copy.wait_recv()
        for j in range(self.lats * 8):
            both[j // 8, j // 2 % 4, j % 2] = (
                part[j, core].astype(F32) + other[j].astype(F32)
            ).astype(BF16)
        self.z_copies = []
        for d in range(1, 4):
            to = lax.rem(z + d, 4)
            self.z_copies.append(self.copy(
                both.at[:, to], self.ref("ring").at[d - 1], send.at[d], recv.at[d],
                lat, to * 4 + x * 2 + core,
            ))
            self.z_copies[-1].start()

    def targets(self):
        lat, z, x, core = self.place
        for l in range(self.lats):
            for xl in range(2):
                mine = jnp.logical_and(lat == self.first + l, x == xl)
                yield l, xl, mine, self.copy(
                    self.ref("last").at[l, xl], self.final.at[lat * 2 + x],
                    self.ref("fsend").at[2 * l + xl], self.final_sem.at[lat * 2 + x],
                    self.first + l, z * 4 + xl * 2 + core,
                )

    def start_last(self):
        lat, z, x, core = self.place
        both, ring, last = self.ref("both"), self.ref("ring"), self.ref("last")
        for copy in self.z_copies:
            copy.wait_recv()
        for l in range(self.lats):
            for xl in range(2):
                total = both[l, z, xl].astype(F32)
                for d in range(3):
                    total += ring[d, l, xl].astype(F32)
                last[l, xl] = total.astype(BF16)
        for l, xl, mine, copy in self.targets():
            @pl.when(jnp.logical_not(mine))
            def _(copy=copy):
                copy.start()

    def finish(self, out):
        lat, z, x, core = self.place
        last = self.ref("last")

        @pl.when(jnp.logical_and(lat >= self.first, lat < self.first + self.lats))
        def _():
            me = lat * 2 + x
            for s in range(16):
                @pl.when(me != s)
                def _():
                    self.copy(
                        last.at[0, 0], self.final.at[s], self.ref("fsend").at[0],
                        self.final_sem.at[s], lat, z * 4 + (1 - x) * 2 + core,
                    ).wait_recv()
            self.final[me] = last[lat - self.first, x]
            groups = self.cols // AUX
            for c in range(groups):
                total = self.final[0, :, c * AUX : (c + 1) * AUX].astype(F32)
                for s in range(1, 16):
                    total += self.final[s, :, c * AUX : (c + 1) * AUX].astype(F32)
                out[pl.ds(c, self.rows, stride=groups), :] = total

    def drain(self):
        self.core_copy.wait_send()
        for copy in self.z_copies:
            copy.wait_send()
        for _, _, mine, copy in self.targets():
            @pl.when(jnp.logical_not(mine))
            def _(copy=copy):
                copy.wait_send()


def body(n_lat, n_lon, given, names, refs):
    r = types.SimpleNamespace(**dict(zip(names, refs)))
    lat, lon = lax.axis_index("lat"), lax.axis_index("lon")
    lat_up, lat_down = lax.rem(lat + 1, n_lat), lax.rem(lat + n_lat - 1, n_lat)
    lon_up, lon_down = lax.rem(lon + 1, n_lon), lax.rem(lon + n_lon - 1, n_lon)
    down = ((lat_down, lon), (lat, lon_down), (lat_down, lon_down))
    up = ((lat_up, lon), (lat, lon_up), (lat_up, lon_up))

    staged = types.SimpleNamespace()
    for i, name in enumerate(given):
        copy = pltpu.make_async_copy(
            getattr(r, "in_" + name), getattr(r, "v_" + name), r.stage_sem.at[i]
        )
        setattr(staged, name, copy)
        copy.start()

    barrier = pltpu.get_barrier_semaphore()
    z, x, core = lon // 4, lon // 2 % 2, lon % 2
    place = (lat, z, x, core)
    sums = types.SimpleNamespace(**{name: Summed(r, name, place) for name in SEGMENTS})
    peers = list(down + up)
    peers += [(lat, lax.rem(z + d, 4) * 4 + x * 2 + core) for d in range(1, 4)]
    peers += [(lax.rem(lat + d, n_lat), lon) for d in range(2, 7)]
    peers += [(lax.rem(lat + d, n_lat), z * 4 + (1 - x) * 2 + core) for d in range(8)]
    for peer in peers:
        pl.semaphore_signal(barrier, inc=1, device_id=peer, device_id_type=MESH)

    def exchange(turn, src, dst, parts, kept, peers):
        copies = []
        for i, (off, size) in enumerate(parts):
            copies.append(
                pltpu.make_async_remote_copy(
                    src_ref=src.at[pl.ds(off - kept, size)],
                    dst_ref=dst.at[pl.ds(off, size)],
                    send_sem=r.send_sem.at[3 * turn + i],
                    recv_sem=r.recv_sem.at[3 * turn + i],
                    device_id=peers[i],
                    device_id_type=MESH,
                )
            )
            copies[-1].start()
        return copies

    def arrived(copies):
        for copy in copies:
            copy.wait_recv()

    def one_hot(name, rows, cols, first=0, base=0):
        wanted = r.v_maps[first : first + rows, name : name + 1] - base
        place = lax.broadcasted_iota(jnp.int32, (rows, cols), 1)
        return jnp.where(place == wanted, 1.0, 0.0)

    def spread(name, rows, cols, first=0, base=0):
        return one_hot(name, rows, cols, first, base).astype(BF16)

    staged.maps.wait()
    staged.tokens.wait()
    send_rows = spread(SEND_ROWS, SLOTS, CELLS)
    mask = r.mask_ids[:, 0, :].astype(F32).astype(BF16)
    flags = r.pad_flags[:, 0, :].astype(F32).astype(BF16)
    row_of, col_of = spread(ROW_OF, CELLS, ROWS), one_hot(COL_OF, CELLS, COLS)
    ids = jnp.sum(dot(row_of, mask) * col_of, axis=-1, keepdims=True)
    flag_rows = jnp.sum(dot(row_of, flags) * col_of, axis=-1, keepdims=True)
    aux = jnp.where(
        lax.broadcasted_iota(jnp.int32, (CELLS, AUX), 1) == 0, ids, 0.0
    ).astype(BF16)
    message = dot(send_rows, r.v_tokens[...]).astype(BF16)
    r.tok_send[:, :WIDE] = message[KEPT:]
    r.tok_recv[:KEPT, :WIDE] = message[:KEPT]
    message = dot(send_rows, aux).astype(BF16)
    r.tok_send[:, WIDE:] = message[KEPT:]
    r.tok_recv[:KEPT, WIDE:] = message[:KEPT]
    pl.semaphore_wait(barrier, len(peers))
    tok = exchange(0, r.tok_send, r.tok_recv, PARTS, KEPT, down)
    staged.cot_fine.wait()
    flagged = (r.v_cot_fine[...].astype(F32) * flag_rows).astype(BF16)
    message = dot(send_rows, flagged).astype(BF16)
    r.cot_send[...] = message[KEPT:]
    r.cot_recv[:KEPT] = message[:KEPT]
    cot = exchange(1, r.cot_send, r.cot_recv, PARTS, KEPT, down)
    staged.cot_coarse.wait()
    message = jnp.zeros((SLOTS_C, COARSE), F32)
    for i in range(6):
        message += dot(spread(SEND_COARSE, SLOTS_C, 12, 0, 12 * i), r.v_cot_coarse[i])
    message = message.astype(BF16)
    r.top_send[:, :COARSE] = message[KEPT_C:]
    r.top_recv[:KEPT_C, :COARSE] = message[:KEPT_C]
    message = dot(spread(SEND_IDS, SLOTS_C, CELLS), aux).astype(BF16)
    r.top_send[:, COARSE:] = message[KEPT_C:]
    r.top_recv[:KEPT_C, COARSE:] = message[:KEPT_C]
    top = exchange(2, r.top_send, r.top_recv, PARTS_C, KEPT_C, down)

    take_windows = spread(TAKE_WINDOWS, CELLS, SLOTS)
    arrived(tok)
    r.ids_fine[...] = dot(take_windows, r.tok_recv[:, WIDE:])
    r.cells[...] = dot(take_windows, r.tok_recv[:, :WIDE])
    (normed,), _ = norm_parts([r.cells[...]])
    r.normed[...] = normed.astype(BF16)
    staged.w_qkv_fine.wait()
    for t in range(3):
        r.packed[:, t * WIDE : (t + 1) * WIDE] = dot(
            r.normed[...], r.v_w_qkv_fine[:, t * WIDE : (t + 1) * WIDE]
        )
    attend(r.packed, r.shares, r.attn, r.ids_fine, 4, WIDE)
    r.mixed[...] = r.attn[...].astype(BF16)
    staged.w_out_fine.wait()
    fine_out = (r.cells[...] + dot(r.mixed[...], r.v_w_out_fine[...])).astype(BF16)
    message = dot(spread(SEND_WINDOWS, SLOTS, CELLS), fine_out).astype(BF16)
    r.out_send[...] = message[KEPT:]
    r.out_recv[:KEPT] = message[:KEPT]
    out = exchange(3, r.out_send, r.out_recv, PARTS, KEPT, down)

    staged.w_out_coarse.wait()
    take_coarse = spread(TAKE_COARSE, WINDOW, SLOTS_C)
    arrived(top)
    r.ids_coarse[...] = dot(take_coarse, r.top_recv[:, COARSE:])
    r.top[...] = dot(take_coarse, r.top_recv[:, :COARSE])
    r.grad_mixed_c[...] = (
        dot_nt(r.top[...].astype(BF16), r.v_w_out_coarse[...]).astype(BF16).astype(F32)
    )

    staged.w_merge.wait()
    arrived(out)
    for k in range(4):
        r.merged[k] = dot(
            spread(TAKE_MERGE, WINDOW, SLOTS, k * WINDOW), r.out_recv[...]
        )
    normed, _ = norm_parts([r.merged[k] for k in range(4)])
    coarse_in = jnp.zeros((WINDOW, COARSE), F32)
    for k in range(4):
        r.normed_merge[k] = normed[k].astype(BF16)
        coarse_in += dot(
            normed[k].astype(BF16), r.v_w_merge[k * WIDE : (k + 1) * WIDE]
        )
    r.coarse_in[...] = coarse_in.astype(BF16).astype(F32)
    (normed,), _ = norm_parts([r.coarse_in[...]])
    normed = normed.astype(BF16)
    staged.w_qkv_coarse.wait()
    for t in range(6):
        r.packed_c[:, t * WIDE : (t + 1) * WIDE] = dot(
            normed, r.v_w_qkv_coarse[:, t * WIDE : (t + 1) * WIDE]
        )
    attend(r.packed_c, r.shares_c, r.attn_c, r.ids_coarse, 1, COARSE)

    top_low = r.top[...].astype(BF16)
    for t in range(2):
        part = dot_tn(r.attn_c[:, t * WIDE : (t + 1) * WIDE].astype(BF16), top_low)
        r.part_out_c[t * 8 : (t + 1) * 8] = part.astype(BF16).reshape(8, 2, 32, COARSE)
    sums.out_c.start_core()
    attend_back(
        r.packed_c, r.shares_c, r.grad_mixed_c, r.grad_packed_c, 1, COARSE
    )
    sums.out_c.start_z()
    grad_normed = jnp.zeros((WINDOW, COARSE), F32)
    for t in range(6):
        part = slice(t * WIDE, (t + 1) * WIDE)
        grad_normed += dot_nt(
            r.grad_packed_c[:, part].astype(BF16), r.v_w_qkv_coarse[:, part]
        )
    normed, scale = norm_parts([r.coarse_in[...]])
    (back,) = norm_parts_back(normed, scale, [grad_normed])
    grad_coarse = (r.top[...] + back).astype(BF16)
    for k in range(4):
        r.grad_merged[k] = dot_nt(grad_coarse, r.v_w_merge[k * WIDE : (k + 1) * WIDE])
    normed, scale = norm_parts([r.merged[k] for k in range(4)])
    back = norm_parts_back(normed, scale, [r.grad_merged[k] for k in range(4)])
    back = jnp.concatenate(back, axis=0).astype(BF16)
    message = dot(spread(TAKE_MERGE_T, SLOTS, CELLS), back).astype(BF16)
    r.back_send[...] = message[KEPT:]
    r.back_recv[:KEPT] = message[:KEPT]
    back = exchange(4, r.back_send, r.back_recv, PARTS, KEPT, up)
    for k in range(4):
        part = dot_tn(r.normed_merge[k], grad_coarse)
        r.part_merge[k * 8 : (k + 1) * 8] = part.astype(BF16).reshape(8, 2, 32, COARSE)
    sums.merge.start_core()
    sums.out_c.start_last()

    arrived(cot)
    r.grad_fine[...] = dot(spread(TAKE_WINDOWS, CELLS, SLOTS), r.cot_recv[...])
    send_windows_t = spread(SEND_WINDOWS_T, CELLS, SLOTS)
    arrived(back)
    r.grad_fine[...] += dot(send_windows_t, r.back_recv[...])
    grad_low = r.grad_fine[...].astype(BF16)
    r.attn[...] = dot_nt(grad_low, r.v_w_out_fine[...]).astype(BF16).astype(F32)
    part = dot_tn(r.mixed[...], grad_low)
    r.part_fine[12:16] = part.astype(BF16).reshape(4, 2, 64, WIDE)
    sums.merge.start_z()
    attend_back(r.packed, r.shares, r.attn, r.grad_packed, 4, WIDE)
    r.grad_low[...] = r.grad_packed[...].astype(BF16)
    for t in range(3):
        part = slice(t * WIDE, (t + 1) * WIDE)
        grads = dot_tn(r.normed[...], r.grad_low[:, part])
        for c in range(4):
            r.mixed_rows[c, pl.ds(t, WIDE, stride=3), :] = grads[:, c * AUX : (c + 1) * AUX]
    for j in range(24):
        for c in range(4):
            r.part_fine[j // 2, j % 2, :, c * AUX : (c + 1) * AUX] = r.mixed_rows[
                c, j * 64 : (j + 1) * 64
            ].astype(BF16)
    sums.fine.start_core()
    sums.merge.start_last()
    grad_normed = jnp.zeros((CELLS, WIDE), F32)
    for t in range(3):
        part = slice(t * WIDE, (t + 1) * WIDE)
        grad_normed += dot_nt(r.grad_low[:, part], r.v_w_qkv_fine[:, part])
    normed, scale = norm_parts([r.cells[...]])
    (back_in,) = norm_parts_back(normed, scale, [grad_normed])
    grad_cells = (r.grad_fine[...] + back_in).astype(BF16)
    message = dot(spread(TAKE_WINDOWS_T, SLOTS, CELLS), grad_cells).astype(BF16)
    r.grad_send[...] = message[KEPT:]
    r.grad_recv[:KEPT] = message[:KEPT]
    grad = exchange(5, r.grad_send, r.grad_recv, PARTS, KEPT, up)
    sums.fine.start_z()
    sums.out_c.finish(r.grad_flat)
    sums.merge.finish(r.grad_flat)
    arrived(grad)
    r.grad_tokens[...] = dot(
        spread(SEND_ROWS_T, CELLS, SLOTS), r.grad_recv[...]
    ).astype(BF16)

    sums.fine.start_last()
    sums.fine.finish(r.grad_flat)
    for segment in (sums.out_c, sums.merge, sums.fine):
        segment.drain()
    for copies in (tok, cot, top, out, back, grad):
        for copy in copies:
            copy.wait_send()


def per_device(n_lat, n_lon, tokens, cot_fine, cot_coarse, mask_ids, pad_flags,
               w_qkv_fine, w_out_fine, w_merge, w_qkv_coarse, w_out_coarse):
    given = dict(
        maps=jnp.asarray(index_maps()),
        tokens=tokens.reshape(CELLS, WIDE),
        cot_fine=cot_fine.reshape(CELLS, WIDE),
        cot_coarse=cot_coarse.reshape(cot_coarse.shape[1:]),
        w_qkv_fine=w_qkv_fine, w_out_fine=w_out_fine, w_merge=w_merge,
        w_qkv_coarse=w_qkv_coarse, w_out_coarse=w_out_coarse,
    )
    small = dict(
        mask_ids=mask_ids.reshape(ROWS, 1, COLS), pad_flags=pad_flags.reshape(ROWS, 1, COLS)
    )
    outs = dict(
        grad_tokens=((CELLS, WIDE), BF16),
        grad_flat=((256, AUX), F32),
    )
    scratch = {"v_" + name: (given[name].shape, given[name].dtype) for name in given}
    scratch.update(
        tok_send=((SLOTS - KEPT, WIDE + AUX), BF16),
        tok_recv=((SLOTS, WIDE + AUX), BF16),
        cot_send=((SLOTS - KEPT, WIDE), BF16),
        cot_recv=((SLOTS, WIDE), BF16),
        top_send=((SLOTS_C - KEPT_C, COARSE + AUX), BF16),
        top_recv=((SLOTS_C, COARSE + AUX), BF16),
        out_send=((SLOTS - KEPT, WIDE), BF16),
        out_recv=((SLOTS, WIDE), BF16),
        back_send=((SLOTS - KEPT, WIDE), BF16),
        back_recv=((SLOTS, WIDE), BF16),
        grad_send=((SLOTS - KEPT, WIDE), BF16),
        grad_recv=((SLOTS, WIDE), BF16),
        ids_fine=((CELLS, AUX), F32),
        ids_coarse=((WINDOW, AUX), F32),
        cells=((CELLS, WIDE), F32),
        normed=((CELLS, WIDE), BF16),
        packed=((CELLS, 3 * WIDE), F32),
        shares=((16, 2 * WINDOW, WINDOW), F32),
        attn=((CELLS, WIDE), F32),
        mixed=((CELLS, WIDE), BF16),
        top=((WINDOW, COARSE), F32),
        grad_mixed_c=((WINDOW, COARSE), F32),
        merged=((4, WINDOW, WIDE), F32),
        normed_merge=((4, WINDOW, WIDE), BF16),
        grad_merged=((4, WINDOW, WIDE), F32),
        coarse_in=((WINDOW, COARSE), F32),
        packed_c=((WINDOW, 3 * COARSE), F32),
        shares_c=((8, 2 * WINDOW, WINDOW), F32),
        attn_c=((WINDOW, COARSE), F32),
        grad_packed_c=((WINDOW, 3 * COARSE), F32),
        grad_fine=((CELLS, WIDE), F32),
        grad_packed=((CELLS, 3 * WIDE), F32),
        grad_low=((CELLS, 3 * WIDE), BF16),
    )
    sems = dict(
        stage_sem=len(given), send_sem=18, recv_sem=18,
        final_recv_fine=16, final_recv_coarse=16,
    )
    scratch.update(
        mixed_rows=((4, 3 * WIDE, AUX), F32),
        final_fine=((16, 64, 512), BF16),
        final_coarse=((16, 32, 1024), BF16),
    )
    for name, (_, lats, rows, cols) in SEGMENTS.items():
        scratch["part_" + name] = ((lats * 8, 2, rows, cols), BF16)
        scratch["core_" + name] = ((lats * 8, rows, cols), BF16)
        scratch["both_" + name] = ((lats, 4, 2, rows, cols), BF16)
        scratch["ring_" + name] = ((3, lats, 2, rows, cols), BF16)
        scratch["last_" + name] = ((lats, 2, rows, cols), BF16)
        sems["ssend_" + name] = 4
        sems["srecv_" + name] = 4
        sems["fsend_" + name] = 2 * lats
    names = (
        ["in_" + name for name in given] + list(small)
        + list(outs) + list(scratch) + list(sems)
    )

    def kernel(*refs):
        body(n_lat, n_lon, list(given), names, refs)

    vmem = pl.BlockSpec(memory_space=pltpu.VMEM)
    results = pl.pallas_call(
        kernel,
        out_shape=[jax.ShapeDtypeStruct(*s) for s in outs.values()],
        in_specs=[pl.BlockSpec(memory_space=pl.ANY)] * len(given) + [vmem, vmem],
        out_specs=[vmem] * len(outs),
        scratch_shapes=[pltpu.VMEM(*s) for s in scratch.values()]
        + [pltpu.SemaphoreType.DMA((n,)) for n in sems.values()],
        compiler_params=pltpu.CompilerParams(
            collective_id=0, has_side_effects=True, vmem_limit_bytes=60 * 2**20
        ),
        name="swin_backward",
    )(*[given[name] for name in given], *small.values())
    return results[0].reshape(tokens.shape), results[1].reshape(-1)


def solution(mesh):
    cells = P(None, "lat", "lon", None)
    ids = P(None, "lat", "lon")
    step = functools.partial(per_device, mesh.shape["lat"], mesh.shape["lon"])
    return jax.shard_map(
        step,
        mesh=mesh,
        in_specs=(cells, cells, cells, ids, ids) + (P(),) * 5,
        out_specs=(cells, P(("lat", "lon"))),
        check_vma=False,
    )
```

```python
import functools
import types

import jax
import jax.numpy as jnp
import numpy as np
from jax import lax
from jax.experimental import pallas as pl
from jax.experimental.pallas import tpu as pltpu
from jax.sharding import PartitionSpec as P

WIN_LAT = 6
WIN_LON = 12
ROWS = 12
COLS = 24
CELLS = ROWS * COLS
WINDOW = WIN_LAT * WIN_LON
WIDE = 512
COARSE = 1024
HEAD = 64
PAIR = 2 * HEAD
AUX = 128
MESH = pl.DeviceIdType.MESH
F32 = jnp.float32
BF16 = jnp.bfloat16

KEPT = 176
PARTS = ((176, 64), (240, 64), (304, 32))
SLOTS = 336
KEPT_C = 32
PARTS_C = ((32, 32), (64, 32), (96, 32))
SLOTS_C = 128


def slot_of(a, b, half_lat, half_lon, cols, offsets):
    if a >= half_lat and b >= half_lon:
        return (a - half_lat) * (cols - half_lon) + b - half_lon
    if b >= half_lon:
        return offsets[0] + a * (cols - half_lon) + b - half_lon
    if a >= half_lat:
        return offsets[1] + (a - half_lat) * half_lon + b
    return offsets[2] + a * half_lon + b


(
    SEND_ROWS, TAKE_WINDOWS, SEND_WINDOWS, TAKE_MERGE,
    SEND_ROWS_T, TAKE_WINDOWS_T, SEND_WINDOWS_T, TAKE_MERGE_T,
    SEND_COARSE, TAKE_COARSE, SEND_IDS, ROW_OF, COL_OF,
) = range(13)


def index_maps():
    fine = [off for off, _ in PARTS]
    coarse = [off for off, _ in PARTS_C]
    table = np.full((SLOTS, AUX), -1, np.int32)
    for a in range(ROWS):
        for b in range(COLS):
            cell = a * COLS + b
            here = slot_of(a, b, 3, 6, COLS, fine)
            came = slot_of((a + 3) % ROWS, (b + 6) % COLS, 3, 6, COLS, fine)
            window = (a // 6 * 2 + b // 12) * WINDOW + a % 6 * 12 + b % 12
            quarter = (a % 2 * 2 + b % 2) * WINDOW + a // 2 * 12 + b // 2
            for name, row, source in (
                (SEND_ROWS, here, cell),
                (TAKE_WINDOWS, window, came),
                (SEND_WINDOWS, here, window),
                (TAKE_MERGE, quarter, came),
            ):
                table[row, name] = source
                table[source, name + SEND_ROWS_T] = row
            table[cell, ROW_OF] = a
            table[cell, COL_OF] = b
    for i in range(6):
        for j in range(12):
            here = slot_of(i, j, 3, 6, 12, coarse)
            came = slot_of((i + 3) % 6, (j + 6) % 12, 3, 6, 12, coarse)
            table[here, SEND_COARSE] = i * 12 + j
            table[i * 12 + j, TAKE_COARSE] = came
            table[here, SEND_IDS] = 2 * i * COLS + 2 * j
    return table


def dot(a, b):
    return jnp.dot(a, b, preferred_element_type=F32)


def dot_nt(a, b):
    return lax.dot_general(a, b, (((1,), (1,)), ((), ())), preferred_element_type=F32)


def dot_tn(a, b):
    return lax.dot_general(a, b, (((0,), (0,)), ((), ())), preferred_element_type=F32)


def norm_parts(parts):
    size = sum(p.shape[-1] for p in parts)
    average = sum(jnp.sum(p, axis=-1, keepdims=True) for p in parts) * (1.0 / size)
    centred = [p - average for p in parts]
    spread = sum(jnp.sum(c * c, axis=-1, keepdims=True) for c in centred) * (1.0 / size)
    scale = lax.rsqrt(spread + 1e-05)
    return [c * scale for c in centred], scale


def norm_parts_back(normed, scale, grads):
    size = sum(p.shape[-1] for p in normed)
    flat = sum(jnp.sum(g, axis=-1, keepdims=True) for g in grads) * (1.0 / size)
    along = sum(
        jnp.sum(g * n, axis=-1, keepdims=True) for g, n in zip(grads, normed)
    ) * (1.0 / size)
    return [scale * (g - flat - n * along) for g, n in zip(grads, normed)]


def first_lanes():
    return lax.broadcasted_iota(jnp.int32, (WINDOW, PAIR), 1) < HEAD


def stacked(x, low):
    return jnp.concatenate([jnp.where(low, x, 0.0), jnp.where(low, 0.0, x)], axis=0)


def split_bf16(x):
    high = x.astype(BF16)
    return high, (x - high.astype(F32)).astype(BF16)


def allowed_of(ids):
    pick = (lax.broadcasted_iota(jnp.int32, (8, AUX), 1) == 0).astype(BF16)
    along = dot_nt(pick, ids.astype(BF16))[0:1]
    same = ids[:, 0:1] == along
    return jnp.concatenate([same, same], axis=0)


def pair_forward(q, k, v, allowed, low):
    q_high, q_low = split_bf16(stacked(q, low))
    k_high, k_low = split_bf16(k)
    scores = dot_nt(q_high, k_high) + dot_nt(q_high, k_low) + dot_nt(q_low, k_high)
    scores = jnp.where(allowed, scores * HEAD**-0.5, -1e30)
    weights = jnp.exp(scores - jnp.max(scores, axis=-1, keepdims=True))
    shares = weights / jnp.sum(weights, axis=-1, keepdims=True)
    result = dot(shares.astype(BF16), v.astype(BF16))
    return shares, jnp.where(low, result[:WINDOW], result[WINDOW:])


def pair_backward(q, k, v, shares, grad, low):
    grad2 = stacked(grad, low).astype(BF16)
    q2 = stacked(q, low).astype(BF16)
    grad_shares = dot_nt(grad2, v.astype(BF16))
    delta = jnp.sum(grad_shares * shares, axis=-1, keepdims=True)
    grad_scores = (shares * (grad_shares - delta) * HEAD**-0.5).astype(BF16)
    grad_q = dot(grad_scores, k.astype(BF16))
    grad_q = jnp.where(low, grad_q[:WINDOW], grad_q[WINDOW:])
    return grad_q, dot_tn(grad_scores, q2), dot_tn(shares.astype(BF16), grad2)


def attend(packed, shares, attn, ids, w, p, pairs):
    rows = slice(w * WINDOW, (w + 1) * WINDOW)
    low = first_lanes()
    q, k, v = (packed[p, rows, t * PAIR : (t + 1) * PAIR] for t in range(3))
    part, result = pair_forward(q, k, v, allowed_of(ids[rows]), low)
    shares[w * pairs + p] = part
    attn[p, rows] = result


def attend_back(packed, shares, grad, grad_packed, w, p, pairs):
    rows = slice(w * WINDOW, (w + 1) * WINDOW)
    low = first_lanes()
    q, k, v = (packed[p, rows, t * PAIR : (t + 1) * PAIR] for t in range(3))
    grads = pair_backward(q, k, v, shares[w * pairs + p], grad[p, rows], low)
    for t in range(3):
        grad_packed[p, rows, t * PAIR : (t + 1) * PAIR] = grads[t]


def over_pairs(first, pairs, step, unit):
    def some(n, carry):
        for i in range(step):
            unit(first + n * step + i)
        return carry

    lax.fori_loop(0, pairs // step, some, 0)


SEGMENTS = dict(
    out_c=(6, 2, dict(z=(0, 1024))),
    merge=(2, 4, dict(z=(0, 384), y=(384, 384), x=(768, 256))),
    fine=(0, 2, dict(z=(0, 512), y=(512, 256), x=(768, 256))),
)
HALF_ROWS = 32


class Place:
    def __init__(self, lat, lon):
        self.lat, self.y, self.x_high = lat, lat % 4, lat // 4
        self.z, self.x_low, self.core = lon // 4, lon // 2 % 2, lon % 2
        self.x = self.x_high * 2 + self.x_low

    def chip(self, x, y, z):
        return (x // 2 * 4 + y, z * 4 + x % 2 * 2 + self.core)

    def shifted(self, dx, dy, dz):
        return self.chip(
            lax.rem(self.x + dx, 4), lax.rem(self.y + dy, 4), lax.rem(self.z + dz, 4)
        )

    def sibling(self):
        return (self.lat, self.z * 4 + self.x_low * 2 + 1 - self.core)


def remote(src, dst, send_sem, recv_sem, peer):
    return pltpu.make_async_remote_copy(
        src_ref=src, dst_ref=dst, send_sem=send_sem, recv_sem=recv_sem,
        device_id=peer, device_id_type=MESH,
    )


class Part:
    def __init__(self, r, name, axis, me):
        self.first, self.lats, parts = SEGMENTS[name]
        self.left, self.cols = parts[axis]
        self.axis, self.me, self.all = axis, me, self.lats == 4
        (self.part, self.ring, self.last, self.final, self.send, self.recv, self.send2,
         self.recv2) = (
            getattr(r, what + name + axis)
            for what in ("pa_", "ri_", "la_", "fi_", "s1_", "r1_", "s2_", "r2_")
        )
        self.kept = kept_shape(self.lats, axis)
        self.holds = True
        if not self.all and axis != "z":
            self.holds = me.y < 2 if axis == "y" else me.x_high == 0
        self.owns = jnp.logical_and(me.lat >= self.first, me.lat < self.first + self.lats)
        self.number = {
            "z": me.lat * 2 + me.x_low, "x": me.y * 4 + me.z, "y": me.x * 4 + me.z,
        }[axis]

    def source(self, to):
        if self.axis == "z":
            return self.part.at[:, to], True
        if self.axis == "x":
            if self.all:
                return self.part.at[pl.ds(to // 2 * 2, 2), :, to % 2], True
            return self.part.at[:, :, to % 2], to // 2 == 0
        if self.all:
            return self.part.at[lax.rem(to + 2, 4)], True
        return self.part.at[to % 2], to < 2

    def mine(self, i, j):
        me = self.me
        if self.axis == "z":
            return self.part[i, me.z, j]
        if self.axis == "x":
            return self.part[(me.x_high * 2 if self.all else 0) + i, j, me.x_low]
        return self.part[lax.rem(me.y + 2, 4) if self.all else me.y % 2, i, j]

    def firsts(self):
        me = self.me
        here = {"x": me.x, "y": me.y, "z": me.z}[self.axis]
        for d in range(1, 4):
            src, some = self.source(lax.rem(here + d, 4))
            shift = [d if self.axis == a else 0 for a in "xyz"]
            yield some, remote(
                src, self.ring.at[d - 1], self.send.at[d - 1], self.recv.at[d - 1],
                me.shifted(*shift),
            )

    def seconds(self):
        me = self.me
        for i in range(self.kept[0]):
            for j in range(self.kept[1]):
                if self.axis == "z":
                    lat, z, x_low = self.first + i, me.z, j
                elif self.axis == "x":
                    lat = me.x_high * 4 + i + 2 * (1 - me.x_high) if self.all else i
                    z, x_low = j, me.x_low
                else:
                    lat = (1 - me.y // 2) * 4 + me.y if self.all else me.y
                    z, x_low = i, j
                same = jnp.logical_and(
                    lat == me.lat, jnp.logical_and(z == me.z, x_low == me.x_low)
                )
                going = jnp.logical_not(same)
                if self.holds is not True:
                    going = jnp.logical_and(going, self.holds)
                n = i * self.kept[1] + j
                yield going, remote(
                    self.last.at[i, j], self.final.at[self.number], self.send2.at[n],
                    self.recv2.at[self.number], (lat, z * 4 + x_low * 2 + me.core),
                )

    def start_first(self):
        for some, copy in self.firsts():
            when(some, copy.start)

    def start_second(self):
        def add():
            for _, copy in self.firsts():
                copy.wait_recv()
            for i in range(self.kept[0]):
                for j in range(self.kept[1]):
                    total = self.mine(i, j).astype(F32)
                    for d in range(3):
                        total += self.ring[d, i, j].astype(F32)
                    self.last[i, j] = total.astype(BF16)

        when(self.holds, add)
        for going, copy in self.seconds():
            when(going, copy.start)

    def finish(self, total):
        me = self.me

        def add():
            for n in range(16):
                copy = remote(
                    self.last.at[0, 0], self.final.at[n], self.send2.at[0],
                    self.recv2.at[n], me.sibling(),
                )
                when(self.number != n, copy.wait_recv)
            if self.axis == "z":
                own = self.last[me.lat - self.first, me.x_low]
            elif self.axis == "x":
                own = self.last[me.y - 2 * (1 - me.x_high) if self.all else me.y, me.z]
            else:
                own = self.last[me.z, me.x_low]
            self.final[self.number] = own
            for c in range(0, self.cols, AUX):
                value = self.final[0, :, c : c + AUX].astype(F32)
                for n in range(1, 16):
                    value += self.final[n, :, c : c + AUX].astype(F32)
                at = self.left + c
                total[at // WIDE, :, at % WIDE : at % WIDE + AUX] = value

        when(self.owns, add)

    def drain(self):
        for some, copy in self.firsts():
            when(some, copy.wait_send)
        for going, copy in self.seconds():
            when(going, copy.wait_send)


def when(condition, step):
    if condition is True:
        step()
    else:
        pl.when(condition)(step)


def kept_shape(lats, axis):
    return {"z": (lats, 2), "x": (2, 4), "y": (4, 2)}[axis]


def put_blocks(parts, group, first, value):
    size = value.shape[-1]
    for part in parts:
        low = max(group * size, part.left)
        high = min((group + 1) * size, part.left + part.cols)
        if low < high:
            for b in range(value.shape[0]):
                n = first + b
                part.part[n // 8, n // 2 % 4, n % 2, :, low - part.left : high - part.left] = (
                    value[b, :, low - group * size : high - group * size]
                )


def eighty(x):
    return jnp.concatenate([x, jnp.zeros((80 - x.shape[0], x.shape[1]), x.dtype)], axis=0)


def body(n_lat, n_lon, given, names, refs):
    r = types.SimpleNamespace(**dict(zip(names, refs)))
    lat, lon = lax.axis_index("lat"), lax.axis_index("lon")
    lat_up, lat_down = lax.rem(lat + 1, n_lat), lax.rem(lat + n_lat - 1, n_lat)
    lon_up, lon_down = lax.rem(lon + 1, n_lon), lax.rem(lon + n_lon - 1, n_lon)
    down = ((lat_down, lon), (lat, lon_down), (lat_down, lon_down))
    up = ((lat_up, lon), (lat, lon_up), (lat_up, lon_up))

    staged = types.SimpleNamespace()
    for i, name in enumerate(given):
        copy = pltpu.make_async_copy(
            getattr(r, "in_" + name), getattr(r, "v_" + name), r.stage_sem.at[i]
        )
        setattr(staged, name, copy)
        copy.start()

    barrier = pltpu.get_barrier_semaphore()
    me = Place(lat, lon)
    core = me.core
    peers = [down[1], down[2], up[1], up[2]]
    for a in range(4):
        for b in range(4):
            peers += [me.shifted(a, b, 0)] if a or b else []
            peers += [me.shifted(0, a, b)] if b else []
            peers += [me.shifted(a, 0, b)] if a and b else []
    for peer in peers:
        pl.semaphore_signal(barrier, inc=1, device_id=peer, device_id_type=MESH)

    sums = {
        name: [Part(r, name, axis, me) for axis in parts]
        for name, (_, _, parts) in SEGMENTS.items()
    }
    out_c, merge, fine = sums.values()

    def exchange(turn, src, dst, parts, kept, peers):
        copies = []
        for i, (off, size) in enumerate(parts):
            copies.append(
                remote(
                    src.at[pl.ds(off - kept, size)], dst.at[pl.ds(off, size)],
                    r.send_sem.at[3 * turn + i], r.recv_sem.at[3 * turn + i], peers[i],
                )
            )
            copies[-1].start()
        return copies

    def arrived(copies):
        for copy in copies:
            copy.wait_recv()

    swaps = []

    def swap(src, dst):
        n = len(swaps)
        swaps.append(remote(src, dst, r.swap_send.at[n], r.swap_recv.at[n], me.sibling()))
        swaps[-1].start()
        return swaps[-1]

    def one_hot(name, rows, cols, first=0, base=0):
        wanted = r.v_maps[first : first + rows, name : name + 1] - base
        place = lax.broadcasted_iota(jnp.int32, (rows, cols), 1)
        return jnp.where(place == wanted, 1.0, 0.0)

    def spread(name, rows, cols, first=0, base=0):
        return one_hot(name, rows, cols, first, base).astype(BF16)

    staged.maps.wait()
    staged.tokens.wait()
    send_rows = spread(SEND_ROWS, SLOTS, CELLS)
    mask = r.mask_ids[:, 0, :].astype(F32).astype(BF16)
    flags = r.pad_flags[:, 0, :].astype(F32).astype(BF16)
    row_of, col_of = spread(ROW_OF, CELLS, ROWS), one_hot(COL_OF, CELLS, COLS)
    ids = jnp.sum(dot(row_of, mask) * col_of, axis=-1, keepdims=True)
    flag_rows = jnp.sum(dot(row_of, flags) * col_of, axis=-1, keepdims=True)
    aux = jnp.where(
        lax.broadcasted_iota(jnp.int32, (CELLS, AUX), 1) == 0, ids, 0.0
    ).astype(BF16)
    message = dot(send_rows, r.v_tokens[...]).astype(BF16)
    r.tok_send[:, :WIDE] = message[KEPT:]
    r.tok_recv[:KEPT, :WIDE] = message[:KEPT]
    message = dot(send_rows, aux).astype(BF16)
    r.tok_send[:, WIDE:] = message[KEPT:]
    r.tok_recv[:KEPT, WIDE:] = message[:KEPT]
    pl.semaphore_wait(barrier, len(peers))
    tok = exchange(0, r.tok_send, r.tok_recv, PARTS, KEPT, down)
    staged.cot_fine.wait()
    flagged = (r.v_cot_fine[...].astype(F32) * flag_rows).astype(BF16)
    message = dot(send_rows, flagged).astype(BF16)
    r.cot_send[...] = message[KEPT:]
    r.cot_recv[:KEPT] = message[:KEPT]
    staged.cot_coarse.wait()
    message = jnp.zeros((SLOTS_C, COARSE), F32)
    for i in range(6):
        message += dot(spread(SEND_COARSE, SLOTS_C, 12, 0, 12 * i), r.v_cot_coarse[i])
    message = message.astype(BF16)
    r.top_send[:, :COARSE] = message[KEPT_C:]
    r.top_recv[:KEPT_C, :COARSE] = message[:KEPT_C]
    message = dot(spread(SEND_IDS, SLOTS_C, CELLS), aux).astype(BF16)
    r.top_send[:, COARSE:] = message[KEPT_C:]
    r.top_recv[:KEPT_C, COARSE:] = message[:KEPT_C]

    def fine_rows(first, count, slots):
        rows = slice(first, first + count)
        take = spread(TAKE_WINDOWS, count, slots, first)
        r.ids_fine[rows] = dot(take, r.tok_recv[:slots, WIDE:])
        r.cells[rows] = dot(take, r.tok_recv[:slots, :WIDE])
        (normed,), _ = norm_parts([r.cells[rows]])
        normed = normed.astype(BF16)
        for t in range(3):
            packed = dot(normed, r.v_w_qkv_fine[:, t * WIDE : (t + 1) * WIDE])
            for p in range(4):
                r.packed[p, rows, t * PAIR : (t + 1) * PAIR] = packed[
                    :, p * PAIR : (p + 1) * PAIR
                ]

    staged.w_qkv_fine.wait()
    fine_rows(0, WINDOW, KEPT)
    over_pairs(0, 4, 4, lambda p: attend(r.packed, r.shares, r.attn, r.ids_fine, 0, p, 4))
    arrived(tok)
    cot = exchange(1, r.cot_send, r.cot_recv, PARTS, KEPT, down)
    top = exchange(2, r.top_send, r.top_recv, PARTS_C, KEPT_C, down)
    fine_rows(WINDOW, CELLS - WINDOW, SLOTS)

    def others(unit):
        def three(p):
            for w in range(3):
                unit(w, p)

        return three

    over_pairs(0, 4, 2, others(
        lambda w, p: attend(r.packed, r.shares, r.attn, r.ids_fine, w + 1, p, 4)
    ))
    mixed = jnp.concatenate([r.attn[p] for p in range(4)], axis=1).astype(BF16)
    r.mixed[0] = mixed
    staged.w_out_fine.wait()
    fine_out = (r.cells[...] + dot(mixed, r.v_w_out_fine[...])).astype(BF16)
    message = dot(spread(SEND_WINDOWS, SLOTS, CELLS), fine_out).astype(BF16)
    r.out_send[...] = message[KEPT:]
    r.out_recv[:KEPT] = message[:KEPT]
    out = exchange(3, r.out_send, r.out_recv, PARTS, KEPT, down)

    (normed,), _ = norm_parts([r.cells[...]])
    r.normed[0] = normed.astype(BF16)
    normed_swap = swap(r.normed.at[0], r.normed.at[1])
    mixed_swap = swap(r.mixed.at[0], r.mixed.at[1])
    staged.w_out_coarse.wait()
    take_coarse = spread(TAKE_COARSE, WINDOW, SLOTS_C)
    arrived(top)
    r.ids_coarse[...] = dot(take_coarse, r.top_recv[:, COARSE:])
    r.top[...] = dot(take_coarse, r.top_recv[:, :COARSE])
    for h in range(2):
        r.top_half[h] = eighty(r.top[:, h * WIDE : (h + 1) * WIDE]).astype(BF16)
    top_swap = swap(r.top_half.at[1 - core], r.top_other)
    grad_mixed = dot_nt(r.top[...].astype(BF16), r.v_w_out_coarse[...])
    for p in range(8):
        r.grad_mixed_c[p] = grad_mixed[:, p * PAIR : (p + 1) * PAIR].astype(BF16).astype(F32)
    arrived(cot)
    r.grad_fine[...] = dot(spread(TAKE_WINDOWS, CELLS, SLOTS), r.cot_recv[...])

    staged.w_merge.wait()
    arrived(out)
    for k in range(4):
        r.merged[k] = dot(spread(TAKE_MERGE, WINDOW, SLOTS, k * WINDOW), r.out_recv[...])
    normed, _ = norm_parts([r.merged[k] for k in range(4)])
    coarse_in = jnp.zeros((WINDOW, COARSE), F32)
    for k in range(4):
        part = eighty(normed[k]).astype(BF16)
        r.normed_merge[0, :, k * WIDE : (k + 1) * WIDE] = part
        coarse_in += dot(
            normed[k].astype(BF16), r.v_w_merge[k * WIDE : (k + 1) * WIDE]
        )
    merge_swap = swap(r.normed_merge.at[0], r.normed_merge.at[1])
    r.coarse_in[...] = coarse_in.astype(BF16).astype(F32)
    (normed,), _ = norm_parts([r.coarse_in[...]])
    normed = normed.astype(BF16)
    staged.w_qkv_coarse.wait()
    for t in range(6):
        packed = dot(normed, r.v_w_qkv_coarse[:, t * WIDE : (t + 1) * WIDE])
        for p in range(4):
            r.packed_c[t % 2 * 4 + p, :, t // 2 * PAIR : (t // 2 + 1) * PAIR] = packed[
                :, p * PAIR : (p + 1) * PAIR
            ]
    over_pairs(0, 8, 4, lambda p: attend(
        r.packed_c, r.shares_c, r.attn_c, r.ids_coarse, 0, p, 8
    ))
    for p in range(8):
        r.mixed_c[0, :, p * PAIR : (p + 1) * PAIR] = eighty(r.attn_c[p]).astype(BF16)
    mixed_c_swap = swap(r.mixed_c.at[0], r.mixed_c.at[1])

    over_pairs(0, 8, 4, lambda p: attend_back(
        r.packed_c, r.shares_c, r.grad_mixed_c, r.grad_packed_c, 0, p, 8
    ))
    mixed_c_swap.wait_recv()
    top_swap.wait_recv()
    both = jnp.concatenate([r.top_half[core], r.top_other[...]], axis=0)
    for t in range(2):
        mixed = r.mixed_c[:, :, t * WIDE : (t + 1) * WIDE].reshape(160, WIDE)
        part = dot_tn(mixed, both).astype(BF16).reshape(8, 2, HALF_ROWS, WIDE)
        for g in range(2):
            put_blocks(out_c, g, t * 8, part[:, g])
    for part in out_c:
        part.start_first()
    grad_normed = jnp.zeros((WINDOW, COARSE), F32)
    for t in range(6):
        grads = jnp.concatenate(
            [
                r.grad_packed_c[t % 2 * 4 + p, :, t // 2 * PAIR : (t // 2 + 1) * PAIR]
                for p in range(4)
            ],
            axis=1,
        ).astype(BF16)
        grad_normed += dot_nt(grads, r.v_w_qkv_coarse[:, t * WIDE : (t + 1) * WIDE])
    normed, scale = norm_parts([r.coarse_in[...]])
    (back,) = norm_parts_back(normed, scale, [grad_normed])
    grad_coarse = r.top[...] + back
    for h in range(2):
        r.grad_coarse[h] = eighty(grad_coarse[:, h * WIDE : (h + 1) * WIDE]).astype(BF16)
    grad_coarse = grad_coarse.astype(BF16)
    coarse_swap = swap(r.grad_coarse.at[1 - core], r.grad_coarse_other)
    for k in range(4):
        r.grad_merged[k] = dot_nt(grad_coarse, r.v_w_merge[k * WIDE : (k + 1) * WIDE])
    normed, scale = norm_parts([r.merged[k] for k in range(4)])
    back = norm_parts_back(normed, scale, [r.grad_merged[k] for k in range(4)])
    back = jnp.concatenate(back, axis=0).astype(BF16)
    message = dot(spread(TAKE_MERGE_T, SLOTS, CELLS), back).astype(BF16)
    r.back_send[...] = message[KEPT:]
    r.back_recv[:KEPT] = message[:KEPT]
    back = exchange(4, r.back_send, r.back_recv, PARTS, KEPT, up)

    merge_swap.wait_recv()
    coarse_swap.wait_recv()
    both = jnp.concatenate([r.grad_coarse[core], r.grad_coarse_other[...]], axis=0)
    for k in range(4):
        normed = r.normed_merge[:, :, k * WIDE : (k + 1) * WIDE].reshape(160, WIDE)
        part = dot_tn(normed, both).astype(BF16).reshape(8, 2, HALF_ROWS, WIDE)
        for g in range(2):
            put_blocks(merge, g, k * 8, part[:, g])
    for part in merge:
        part.start_first()

    def fine_rows_back(first, count, slots):
        rows = slice(first, first + count)
        r.grad_fine[rows] += dot(
            spread(SEND_WINDOWS_T, count, slots, first), r.back_recv[:slots]
        )
        low = r.grad_fine[rows].astype(BF16)
        grad_mixed = dot_nt(low, r.v_w_out_fine[...])
        for p in range(4):
            r.attn[p, rows] = grad_mixed[:, p * PAIR : (p + 1) * PAIR].astype(BF16).astype(F32)

    def window_back(w, p):
        attend_back(r.packed, r.shares, r.attn, r.grad_packed, w, p, 4)

    fine_rows_back(3 * WINDOW, WINDOW, KEPT)
    over_pairs(0, 4, 4, lambda p: window_back(3, p))
    arrived(back)
    fine_rows_back(0, 3 * WINDOW, SLOTS)
    for h in range(2):
        r.grad_low[h] = r.grad_fine[:, h * 256 : (h + 1) * 256].astype(BF16)
    low_swap = swap(r.grad_low.at[1 - core], r.grad_low_other)
    other = 2 * (1 - core)
    over_pairs(other, 2, 2, others(window_back))
    for i in range(2):
        r.grad_pair[other + i] = r.grad_packed[other + i].astype(BF16)
    pair_swap = swap(r.grad_pair.at[pl.ds(other, 2)], r.grad_pair_other)
    for part in out_c:
        part.start_second()
    own = 2 * core
    over_pairs(own, 2, 2, others(window_back))
    for i in range(2):
        r.grad_pair[own + i] = r.grad_packed[own + i].astype(BF16)
    mixed_swap.wait_recv()
    low_swap.wait_recv()
    both = jnp.concatenate([r.grad_low[core], r.grad_low_other[...]], axis=0)
    part = dot_tn(r.mixed[...].reshape(2 * CELLS, WIDE), both).astype(BF16)
    part = part.reshape(4, 4, HALF_ROWS, 256)
    for g in range(4):
        put_blocks(fine, g, 12, part[:, g])
    normed_swap.wait_recv()
    pair_swap.wait_recv()
    for i in range(2):
        both = jnp.concatenate([r.grad_pair[own + i], r.grad_pair_other[i]], axis=0)
        grads = dot_tn(r.normed[...].reshape(2 * CELLS, WIDE), both)
        for t in range(3):
            r.mixed_rows[i, pl.ds(t, WIDE, stride=3), :] = grads[:, t * PAIR : (t + 1) * PAIR]
    for b in range(12):
        rows = [
            jnp.concatenate(
                [r.mixed_rows[i, pl.ds(b * 128 + g * 32, 32), :] for i in range(2)], axis=1
            ).astype(BF16)
            for g in range(4)
        ]
        for g in range(4):
            put_blocks(fine, g, b, rows[g][None])
    for part in fine:
        part.start_first()
    for part in merge:
        part.start_second()
    grad_normed = jnp.zeros((CELLS, WIDE), F32)
    for t in range(3):
        grads = jnp.concatenate(
            [r.grad_pair[p, :, t * PAIR : (t + 1) * PAIR] for p in range(4)], axis=1
        )
        grad_normed += dot_nt(grads, r.v_w_qkv_fine[:, t * WIDE : (t + 1) * WIDE])
    normed, scale = norm_parts([r.cells[...]])
    (back_in,) = norm_parts_back(normed, scale, [grad_normed])
    grad_cells = (r.grad_fine[...] + back_in).astype(BF16)
    message = dot(spread(TAKE_WINDOWS_T, SLOTS, CELLS), grad_cells).astype(BF16)
    r.grad_send[...] = message[KEPT:]
    r.grad_recv[:KEPT] = message[:KEPT]
    grad = exchange(5, r.grad_send, r.grad_recv, PARTS, KEPT, up)
    for part in out_c:
        part.finish(r.total)
    for part in fine:
        part.start_second()
    arrived(grad)
    r.grad_tokens[...] = dot(
        spread(SEND_ROWS_T, CELLS, SLOTS), r.grad_recv[...]
    ).astype(BF16)
    for part in merge + fine:
        part.finish(r.total)

    total_swap = swap(r.total.at[1 - core], r.total_other)
    total_swap.wait_recv()
    here, there = r.total[core], r.total_other[...]
    halves = [jnp.where(core == 0, here, there), jnp.where(core == 0, there, here)]

    def out_fine():
        for h in range(2):
            for c in range(4):
                r.grad_flat[pl.ds(c // 2 * 128 + 2 * h + c % 2, 32, stride=4), :] = halves[h][
                    :, c * AUX : (c + 1) * AUX
                ]

    def out_coarse():
        for h in range(2):
            for c in range(4):
                r.grad_flat[pl.ds(4 * h + c, 32, stride=8), :] = halves[h][
                    :, c * AUX : (c + 1) * AUX
                ]

    when(me.lat < 2, out_fine)
    when(me.lat >= 2, out_coarse)
    for part in out_c + merge + fine:
        part.drain()
    for copies in (tok, cot, top, out, back, grad, swaps):
        for copy in copies:
            copy.wait_send()


def per_device(n_lat, n_lon, tokens, cot_fine, cot_coarse, mask_ids, pad_flags,
               w_qkv_fine, w_out_fine, w_merge, w_qkv_coarse, w_out_coarse):
    given = dict(
        maps=jnp.asarray(index_maps()),
        tokens=tokens.reshape(CELLS, WIDE),
        cot_fine=cot_fine.reshape(CELLS, WIDE),
        cot_coarse=cot_coarse.reshape(cot_coarse.shape[1:]),
        w_qkv_fine=w_qkv_fine, w_out_fine=w_out_fine, w_merge=w_merge,
        w_qkv_coarse=w_qkv_coarse, w_out_coarse=w_out_coarse,
    )
    small = dict(
        mask_ids=mask_ids.reshape(ROWS, 1, COLS), pad_flags=pad_flags.reshape(ROWS, 1, COLS)
    )
    outs = dict(
        grad_tokens=((CELLS, WIDE), BF16),
        grad_flat=((256, AUX), F32),
    )
    scratch = {"v_" + name: (given[name].shape, given[name].dtype) for name in given}
    scratch.update(
        tok_send=((SLOTS - KEPT, WIDE + AUX), BF16),
        tok_recv=((SLOTS, WIDE + AUX), BF16),
        cot_send=((SLOTS - KEPT, WIDE), BF16),
        cot_recv=((SLOTS, WIDE), BF16),
        top_send=((SLOTS_C - KEPT_C, COARSE + AUX), BF16),
        top_recv=((SLOTS_C, COARSE + AUX), BF16),
        out_send=((SLOTS - KEPT, WIDE), BF16),
        out_recv=((SLOTS, WIDE), BF16),
        back_send=((SLOTS - KEPT, WIDE), BF16),
        back_recv=((SLOTS, WIDE), BF16),
        grad_send=((SLOTS - KEPT, WIDE), BF16),
        grad_recv=((SLOTS, WIDE), BF16),
        ids_fine=((CELLS, AUX), F32),
        ids_coarse=((WINDOW, AUX), F32),
        cells=((CELLS, WIDE), F32),
        normed=((2, CELLS, WIDE), BF16),
        packed=((4, CELLS, 3 * PAIR), F32),
        shares=((16, 2 * WINDOW, WINDOW), F32),
        attn=((4, CELLS, PAIR), F32),
        mixed=((2, CELLS, WIDE), BF16),
        top=((WINDOW, COARSE), F32),
        top_half=((2, 80, WIDE), BF16),
        top_other=((80, WIDE), BF16),
        grad_mixed_c=((8, WINDOW, PAIR), F32),
        merged=((4, WINDOW, WIDE), F32),
        normed_merge=((2, 80, 4 * WIDE), BF16),
        grad_merged=((4, WINDOW, WIDE), F32),
        coarse_in=((WINDOW, COARSE), F32),
        packed_c=((8, WINDOW, 3 * PAIR), F32),
        shares_c=((8, 2 * WINDOW, WINDOW), F32),
        attn_c=((8, WINDOW, PAIR), F32),
        mixed_c=((2, 80, COARSE), BF16),
        grad_packed_c=((8, WINDOW, 3 * PAIR), F32),
        grad_coarse=((2, 80, WIDE), BF16),
        grad_coarse_other=((80, WIDE), BF16),
        grad_fine=((CELLS, WIDE), F32),
        grad_low=((2, CELLS, 256), BF16),
        grad_low_other=((CELLS, 256), BF16),
        grad_packed=((4, CELLS, 3 * PAIR), F32),
        grad_pair=((4, CELLS, 3 * PAIR), BF16),
        grad_pair_other=((2, CELLS, 3 * PAIR), BF16),
        mixed_rows=((2, 3 * WIDE, AUX), F32),
        total=((2, HALF_ROWS, WIDE), F32),
        total_other=((HALF_ROWS, WIDE), F32),
    )
    sems = dict(
        stage_sem=len(given), send_sem=18, recv_sem=18, swap_send=16, swap_recv=16
    )
    for name, (_, lats, parts) in SEGMENTS.items():
        for axis, (_, cols) in parts.items():
            kept = kept_shape(lats, axis)
            block = (HALF_ROWS, cols)
            scratch["pa_" + name + axis] = ((lats, 4, 2) + block, BF16)
            scratch["ri_" + name + axis] = ((3,) + kept + block, BF16)
            scratch["la_" + name + axis] = (kept + block, BF16)
            scratch["fi_" + name + axis] = ((16,) + block, BF16)
            sems["s1_" + name + axis] = sems["r1_" + name + axis] = 3
            sems["s2_" + name + axis], sems["r2_" + name + axis] = 8, 16
    names = (
        ["in_" + name for name in given] + list(small)
        + list(outs) + list(scratch) + list(sems)
    )

    def kernel(*refs):
        body(n_lat, n_lon, list(given), names, refs)

    vmem = pl.BlockSpec(memory_space=pltpu.VMEM)
    results = pl.pallas_call(
        kernel,
        out_shape=[jax.ShapeDtypeStruct(*s) for s in outs.values()],
        in_specs=[pl.BlockSpec(memory_space=pl.ANY)] * len(given) + [vmem, vmem],
        out_specs=[vmem] * len(outs),
        scratch_shapes=[pltpu.VMEM(*s) for s in scratch.values()]
        + [pltpu.SemaphoreType.DMA((n,)) for n in sems.values()],
        compiler_params=pltpu.CompilerParams(
            collective_id=0, has_side_effects=True, vmem_limit_bytes=60 * 2**20
        ),
        name="swin_backward",
    )(*[given[name] for name in given], *small.values())
    return results[0].reshape(tokens.shape), results[1].reshape(-1)


def solution(mesh):
    cells = P(None, "lat", "lon", None)
    ids = P(None, "lat", "lon")
    step = functools.partial(per_device, mesh.shape["lat"], mesh.shape["lon"])
    return jax.shard_map(
        step,
        mesh=mesh,
        in_specs=(cells, cells, cells, ids, ids) + (P(),) * 5,
        out_specs=(cells, P(("lat", "lon"))),
        check_vma=False,
    )
```

```python
import functools
import types

import jax
import jax.numpy as jnp
import numpy as np
from jax import lax
from jax.experimental import pallas as pl
from jax.experimental.pallas import tpu as pltpu
from jax.sharding import PartitionSpec as P

WIN_LAT = 6
WIN_LON = 12
ROWS = 12
COLS = 24
CELLS = ROWS * COLS
WINDOW = WIN_LAT * WIN_LON
WIDE = 512
COARSE = 1024
HEAD = 64
PAIR = 2 * HEAD
AUX = 128
MESH = pl.DeviceIdType.MESH
F32 = jnp.float32
BF16 = jnp.bfloat16

KEPT = 176
PARTS = ((176, 64), (240, 64), (304, 32))
SLOTS = 336
KEPT_C = 32
PARTS_C = ((32, 32), (64, 32), (96, 32))
SLOTS_C = 128


def slot_of(a, b, half_lat, half_lon, cols, offsets):
    if a >= half_lat and b >= half_lon:
        return (a - half_lat) * (cols - half_lon) + b - half_lon
    if b >= half_lon:
        return offsets[0] + a * (cols - half_lon) + b - half_lon
    if a >= half_lat:
        return offsets[1] + (a - half_lat) * half_lon + b
    return offsets[2] + a * half_lon + b


(
    SEND_ROWS, TAKE_WINDOWS, SEND_WINDOWS, TAKE_MERGE,
    SEND_ROWS_T, TAKE_WINDOWS_T, SEND_WINDOWS_T, TAKE_MERGE_T,
    SEND_COARSE, TAKE_COARSE, SEND_IDS, ROW_OF, COL_OF,
) = range(13)


def index_maps():
    fine = [off for off, _ in PARTS]
    coarse = [off for off, _ in PARTS_C]
    table = np.full((SLOTS, AUX), -1, np.int32)
    for a in range(ROWS):
        for b in range(COLS):
            cell = a * COLS + b
            here = slot_of(a, b, 3, 6, COLS, fine)
            came = slot_of((a + 3) % ROWS, (b + 6) % COLS, 3, 6, COLS, fine)
            window = (a // 6 * 2 + b // 12) * WINDOW + a % 6 * 12 + b % 12
            quarter = (a % 2 * 2 + b % 2) * WINDOW + a // 2 * 12 + b // 2
            for name, row, source in (
                (SEND_ROWS, here, cell),
                (TAKE_WINDOWS, window, came),
                (SEND_WINDOWS, here, window),
                (TAKE_MERGE, quarter, came),
            ):
                table[row, name] = source
                table[source, name + SEND_ROWS_T] = row
            table[cell, ROW_OF] = a
            table[cell, COL_OF] = b
    for i in range(6):
        for j in range(12):
            here = slot_of(i, j, 3, 6, 12, coarse)
            came = slot_of((i + 3) % 6, (j + 6) % 12, 3, 6, 12, coarse)
            table[here, SEND_COARSE] = i * 12 + j
            table[i * 12 + j, TAKE_COARSE] = came
            table[here, SEND_IDS] = 2 * i * COLS + 2 * j
    return table


def dot(a, b):
    return jnp.dot(a, b, preferred_element_type=F32)


def dot_nt(a, b):
    return lax.dot_general(a, b, (((1,), (1,)), ((), ())), preferred_element_type=F32)


def dot_tn(a, b):
    return lax.dot_general(a, b, (((0,), (0,)), ((), ())), preferred_element_type=F32)


def norm_parts(parts):
    size = sum(p.shape[-1] for p in parts)
    average = sum(jnp.sum(p, axis=-1, keepdims=True) for p in parts) * (1.0 / size)
    centred = [p - average for p in parts]
    spread = sum(jnp.sum(c * c, axis=-1, keepdims=True) for c in centred) * (1.0 / size)
    scale = lax.rsqrt(spread + 1e-05)
    return [c * scale for c in centred], scale


def norm_parts_back(normed, scale, grads):
    size = sum(p.shape[-1] for p in normed)
    flat = sum(jnp.sum(g, axis=-1, keepdims=True) for g in grads) * (1.0 / size)
    along = sum(
        jnp.sum(g * n, axis=-1, keepdims=True) for g, n in zip(grads, normed)
    ) * (1.0 / size)
    return [scale * (g - flat - n * along) for g, n in zip(grads, normed)]


def first_lanes():
    return lax.broadcasted_iota(jnp.int32, (WINDOW, PAIR), 1) < HEAD


def stacked(x, low):
    return jnp.concatenate([jnp.where(low, x, 0.0), jnp.where(low, 0.0, x)], axis=0)


def split_bf16(x):
    high = x.astype(BF16)
    return high, (x - high.astype(F32)).astype(BF16)


def allowed_of(ids):
    pick = (lax.broadcasted_iota(jnp.int32, (8, AUX), 1) == 0).astype(BF16)
    along = dot_nt(pick, ids.astype(BF16))[0:1]
    same = jnp.where(ids[:, 0:1] == along, 1.0, 0.0)
    return jnp.concatenate([same, same], axis=0)


def pair_forward(q, k, v, allowed, low):
    q_high, q_low = split_bf16(stacked(q * HEAD**-0.5, low))
    k_high, k_low = split_bf16(k)
    scores = dot_nt(
        jnp.concatenate([q_high, q_low], axis=1), jnp.concatenate([k_high, k_high], axis=1)
    ) + dot_nt(q_high, k_low)
    scores = jnp.where(allowed > 0.0, scores, -1e30)
    weights = jnp.exp(scores - jnp.max(scores, axis=-1, keepdims=True)).astype(BF16)
    result = dot(weights, jnp.concatenate([v.astype(BF16), jnp.ones_like(v, BF16)], axis=1))
    scale = 1.0 / result[:, PAIR:]
    result = result[:, :PAIR] * scale
    shares = weights.astype(F32) * scale[:, :WINDOW]
    return shares, jnp.where(low, result[:WINDOW], result[WINDOW:])


def pair_backward(q, k, v, shares, grad, low):
    grad2 = stacked(grad, low).astype(BF16)
    q2 = stacked(q, low).astype(BF16)
    grad_shares = dot_nt(grad2, v.astype(BF16))
    delta = jnp.sum(grad_shares * shares, axis=-1, keepdims=True)
    grad_scores = (shares * (grad_shares - delta) * HEAD**-0.5).astype(BF16)
    grad_q = dot(grad_scores, k.astype(BF16))
    grad_q = jnp.where(low, grad_q[:WINDOW], grad_q[WINDOW:])
    return grad_q, dot_tn(grad_scores, q2), dot_tn(shares.astype(BF16), grad2)


def attend(packed, shares, attn, allowed, w, p, pairs):
    rows = slice(w * WINDOW, (w + 1) * WINDOW)
    low = first_lanes()
    q, k, v = (packed[p, rows, t * PAIR : (t + 1) * PAIR] for t in range(3))
    part, result = pair_forward(q, k, v, allowed[w], low)
    shares[w * pairs + p] = part
    attn[p, rows] = result


def attend_back(packed, shares, grad, grad_packed, w, p, pairs):
    rows = slice(w * WINDOW, (w + 1) * WINDOW)
    low = first_lanes()
    q, k, v = (packed[p, rows, t * PAIR : (t + 1) * PAIR] for t in range(3))
    grads = pair_backward(q, k, v, shares[w * pairs + p], grad[p, rows], low)
    for t in range(3):
        grad_packed[p, rows, t * PAIR : (t + 1) * PAIR] = grads[t]


def over_pairs(first, pairs, step, unit):
    def some(n, carry):
        for i in range(step):
            unit(first + n * step + i)
        return carry

    lax.fori_loop(0, pairs // step, some, 0)


SEGMENTS = dict(
    out_c=(6, 2, dict(z=(0, 512), y=(512, 256), x=(768, 256))),
    merge=(2, 4, dict(z=(0, 384), y=(384, 384), x=(768, 256))),
    fine=(0, 2, dict(z=(0, 512), y=(512, 256), x=(768, 256))),
)
HALF_ROWS = 32


class Place:
    def __init__(self, lat, lon):
        self.lat, self.y, self.x_high = lat, lat % 4, lat // 4
        self.z, self.x_low, self.core = lon // 4, lon // 2 % 2, lon % 2
        self.x = self.x_high * 2 + self.x_low

    def chip(self, x, y, z):
        return (x // 2 * 4 + y, z * 4 + x % 2 * 2 + self.core)

    def shifted(self, dx, dy, dz):
        return self.chip(
            lax.rem(self.x + dx, 4), lax.rem(self.y + dy, 4), lax.rem(self.z + dz, 4)
        )

    def sibling(self):
        return (self.lat, self.z * 4 + self.x_low * 2 + 1 - self.core)


def remote(src, dst, send_sem, recv_sem, peer):
    return pltpu.make_async_remote_copy(
        src_ref=src, dst_ref=dst, send_sem=send_sem, recv_sem=recv_sem,
        device_id=peer, device_id_type=MESH,
    )


class Part:
    def __init__(self, r, name, axis, me):
        self.first, self.lats, parts = SEGMENTS[name]
        self.left, self.cols = parts[axis]
        self.axis, self.me, self.all = axis, me, self.lats == 4
        (self.part, self.ring, self.last, self.final, self.send, self.recv, self.send2,
         self.recv2) = (
            getattr(r, what + name + axis)
            for what in ("pa_", "ri_", "la_", "fi_", "s1_", "r1_", "s2_", "r2_")
        )
        self.kept = kept_shape(self.lats, axis)
        self.holds = True
        if not self.all and axis != "z":
            self.holds = self.among(me.y if axis == "y" else me.x)
        self.owns = jnp.logical_and(me.lat >= self.first, me.lat < self.first + self.lats)
        self.number = {
            "z": me.lat * 2 + me.x_low, "x": me.y * 4 + me.z, "y": me.x * 4 + me.z,
        }[axis]

    def among(self, index):
        return index // 2 == self.first // 4

    def source(self, to):
        if self.axis == "z":
            return self.part.at[:, to], True
        if self.axis == "x":
            if self.all:
                return self.part.at[pl.ds(to // 2 * 2, 2), :, to % 2], True
            return self.part.at[:, :, to % 2], self.among(to)
        if self.all:
            return self.part.at[lax.rem(to + 2, 4)], True
        return self.part.at[to % 2], self.among(to)

    def mine(self, i, j):
        me = self.me
        if self.axis == "z":
            return self.part[i, me.z, j]
        if self.axis == "x":
            return self.part[(me.x_high * 2 if self.all else 0) + i, j, me.x_low]
        return self.part[lax.rem(me.y + 2, 4) if self.all else me.y % 2, i, j]

    def firsts(self):
        me = self.me
        here = {"x": me.x, "y": me.y, "z": me.z}[self.axis]
        for d in range(1, 4):
            src, some = self.source(lax.rem(here + d, 4))
            shift = [d if self.axis == a else 0 for a in "xyz"]
            yield some, remote(
                src, self.ring.at[d - 1], self.send.at[d - 1], self.recv.at[d - 1],
                me.shifted(*shift),
            )

    def seconds(self):
        me = self.me
        for i in range(self.kept[0]):
            for j in range(self.kept[1]):
                if self.axis == "z":
                    lat, z, x_low = self.first + i, me.z, j
                elif self.axis == "x":
                    lat = me.x_high * 4 + i + 2 * (1 - me.x_high) if self.all else self.first + i
                    z, x_low = j, me.x_low
                else:
                    lat = (1 - me.y // 2) * 4 + me.y if self.all else self.first + me.y % 2
                    z, x_low = i, j
                same = jnp.logical_and(
                    lat == me.lat, jnp.logical_and(z == me.z, x_low == me.x_low)
                )
                going = jnp.logical_not(same)
                if self.holds is not True:
                    going = jnp.logical_and(going, self.holds)
                n = i * self.kept[1] + j
                yield going, remote(
                    self.last.at[i, j], self.final.at[self.number], self.send2.at[n],
                    self.recv2.at[self.number], (lat, z * 4 + x_low * 2 + me.core),
                )

    def start_first(self):
        for some, copy in self.firsts():
            when(some, copy.start)

    def start_second(self):
        def add():
            for _, copy in self.firsts():
                copy.wait_recv()
            for i in range(self.kept[0]):
                for j in range(self.kept[1]):
                    total = self.mine(i, j).astype(F32)
                    for d in range(3):
                        total += self.ring[d, i, j].astype(F32)
                    self.last[i, j] = total.astype(BF16)

        when(self.holds, add)
        for going, copy in self.seconds():
            when(going, copy.start)

    def finish(self, total):
        me = self.me

        def add():
            for n in range(16):
                copy = remote(
                    self.last.at[0, 0], self.final.at[n], self.send2.at[0],
                    self.recv2.at[n], me.sibling(),
                )
                when(self.number != n, copy.wait_recv)
            if self.axis == "z":
                own = self.last[me.lat - self.first, me.x_low]
            elif self.axis == "x":
                own = self.last[me.y - 2 * (1 - me.x_high) if self.all else me.y % 2, me.z]
            else:
                own = self.last[me.z, me.x_low]
            self.final[self.number] = own
            for c in range(0, self.cols, AUX):
                value = self.final[0, :, c : c + AUX].astype(F32)
                for n in range(1, 16):
                    value += self.final[n, :, c : c + AUX].astype(F32)
                at = self.left + c
                total[at // WIDE, :, at % WIDE : at % WIDE + AUX] = value

        when(self.owns, add)

    def drain(self):
        for some, copy in self.firsts():
            when(some, copy.wait_send)
        for going, copy in self.seconds():
            when(going, copy.wait_send)


def when(condition, step):
    if condition is True:
        step()
    else:
        pl.when(condition)(step)


def kept_shape(lats, axis):
    return {"z": (lats, 2), "x": (2, 4), "y": (4, 2)}[axis]


def put_blocks(parts, group, first, value):
    size = value.shape[-1]
    for part in parts:
        low = max(group * size, part.left)
        high = min((group + 1) * size, part.left + part.cols)
        if low < high:
            for b in range(value.shape[0]):
                n = first + b
                part.part[n // 8, n // 2 % 4, n % 2, :, low - part.left : high - part.left] = (
                    value[b, :, low - group * size : high - group * size]
                )


def eighty(x):
    return jnp.concatenate([x, jnp.zeros((80 - x.shape[0], x.shape[1]), x.dtype)], axis=0)


def body(n_lat, n_lon, given, names, refs):
    r = types.SimpleNamespace(**dict(zip(names, refs)))
    lat, lon = lax.axis_index("lat"), lax.axis_index("lon")
    lat_up, lat_down = lax.rem(lat + 1, n_lat), lax.rem(lat + n_lat - 1, n_lat)
    lon_up, lon_down = lax.rem(lon + 1, n_lon), lax.rem(lon + n_lon - 1, n_lon)
    down = ((lat_down, lon), (lat, lon_down), (lat_down, lon_down))
    up = ((lat_up, lon), (lat, lon_up), (lat_up, lon_up))

    staged = types.SimpleNamespace()
    for i, name in enumerate(given):
        copy = pltpu.make_async_copy(
            getattr(r, "in_" + name), getattr(r, "v_" + name), r.stage_sem.at[i]
        )
        setattr(staged, name, copy)
        copy.start()

    barrier = pltpu.get_barrier_semaphore()
    me = Place(lat, lon)
    core = me.core
    peers = [down[1], down[2], up[1], up[2]]
    for a in range(4):
        for b in range(4):
            peers += [me.shifted(a, b, 0)] if a or b else []
            peers += [me.shifted(0, a, b)] if b else []
            peers += [me.shifted(a, 0, b)] if a and b else []
    for peer in peers:
        pl.semaphore_signal(barrier, inc=1, device_id=peer, device_id_type=MESH)

    sums = {
        name: [Part(r, name, axis, me) for axis in parts]
        for name, (_, _, parts) in SEGMENTS.items()
    }
    out_c, merge, fine = sums.values()

    def exchange(turn, src, dst, parts, kept, peers, which=(0, 1, 2)):
        copies = []
        for i in which:
            off, size = parts[i]
            copies.append(
                remote(
                    src.at[pl.ds(off - kept, size)], dst.at[pl.ds(off, size)],
                    r.send_sem.at[3 * turn + i], r.recv_sem.at[3 * turn + i], peers[i],
                )
            )
            copies[-1].start()
        return copies

    def arrived(copies):
        for copy in copies:
            copy.wait_recv()

    swaps = []

    def swap(src, dst):
        n = len(swaps)
        swaps.append(remote(src, dst, r.swap_send.at[n], r.swap_recv.at[n], me.sibling()))
        swaps[-1].start()
        return swaps[-1]

    def one_hot(name, rows, cols, first=0, base=0):
        wanted = r.v_maps[first : first + rows, name : name + 1] - base
        place = lax.broadcasted_iota(jnp.int32, (rows, cols), 1)
        return jnp.where(place == wanted, 1.0, 0.0)

    def spread(name, rows, cols, first=0, base=0):
        return one_hot(name, rows, cols, first, base).astype(BF16)

    staged.maps.wait()
    staged.tokens.wait()
    send_rows = spread(SEND_ROWS, SLOTS, CELLS)
    mask = r.mask_ids[:, 0, :].astype(F32).astype(BF16)
    flags = r.pad_flags[:, 0, :].astype(F32).astype(BF16)
    row_of, col_of = spread(ROW_OF, CELLS, ROWS), one_hot(COL_OF, CELLS, COLS)
    ids = jnp.sum(dot(row_of, mask) * col_of, axis=-1, keepdims=True)
    flag_rows = jnp.sum(dot(row_of, flags) * col_of, axis=-1, keepdims=True)
    aux = jnp.where(
        lax.broadcasted_iota(jnp.int32, (CELLS, AUX), 1) == 0, ids, 0.0
    ).astype(BF16)
    message = dot(send_rows, r.v_tokens[...]).astype(BF16)
    r.tok_send[:, :WIDE] = message[KEPT:]
    r.tok_recv[:KEPT, :WIDE] = message[:KEPT]
    message = dot(send_rows, aux).astype(BF16)
    r.tok_send[:, WIDE:] = message[KEPT:]
    r.tok_recv[:KEPT, WIDE:] = message[:KEPT]
    pl.semaphore_wait(barrier, len(peers))
    tok = exchange(0, r.tok_send, r.tok_recv, PARTS, KEPT, down)
    staged.cot_fine.wait()
    flagged = (r.v_cot_fine[...].astype(F32) * flag_rows).astype(BF16)
    message = dot(send_rows, flagged).astype(BF16)
    r.cot_send[...] = message[KEPT:]
    r.cot_recv[:KEPT] = message[:KEPT]
    staged.cot_coarse.wait()
    message = jnp.zeros((SLOTS_C, COARSE), F32)
    for i in range(6):
        message += dot(spread(SEND_COARSE, SLOTS_C, 12, 0, 12 * i), r.v_cot_coarse[i])
    message = message.astype(BF16)
    r.top_send[:, :COARSE] = message[KEPT_C:]
    r.top_recv[:KEPT_C, :COARSE] = message[:KEPT_C]
    message = dot(spread(SEND_IDS, SLOTS_C, CELLS), aux).astype(BF16)
    r.top_send[:, COARSE:] = message[KEPT_C:]
    r.top_recv[:KEPT_C, COARSE:] = message[:KEPT_C]

    def taken(name, first, count, source, ranges, cols):
        return sum(
            dot(spread(name, count, size, first, off), source[off : off + size, cols])
            for off, size in ranges
        )

    def fine_rows(first, count, ranges):
        rows = slice(first, first + count)
        ids = taken(TAKE_WINDOWS, first, count, r.tok_recv, ranges, slice(WIDE, WIDE + AUX))
        for w in range(count // WINDOW):
            r.allowed[first // WINDOW + w] = allowed_of(ids[w * WINDOW : (w + 1) * WINDOW])
        r.cells[rows] = taken(
            TAKE_WINDOWS, first, count, r.tok_recv, ranges, slice(0, WIDE)
        )
        (normed,), _ = norm_parts([r.cells[rows]])
        normed = normed.astype(BF16)
        for t in range(3):
            packed = dot(normed, r.v_w_qkv_fine[:, t * WIDE : (t + 1) * WIDE])
            for p in range(4):
                r.packed[p, rows, t * PAIR : (t + 1) * PAIR] = packed[
                    :, p * PAIR : (p + 1) * PAIR
                ]

    def fine_attend(w, p):
        attend(r.packed, r.shares, r.attn, r.allowed, w, p, 4)

    def fine_result(first, count):
        rows = slice(first, first + count)
        mixed = jnp.concatenate([r.attn[p, rows] for p in range(4)], axis=1).astype(BF16)
        r.mixed[0, rows] = mixed
        fine_out = r.cells[rows] + dot(mixed, r.v_w_out_fine[...])
        r.fine_out[rows] = fine_out.astype(BF16)

    def fine_message(rows, slots):
        first, size = slots
        return dot(spread(SEND_WINDOWS, size, rows, first), r.fine_out[:rows]).astype(BF16)

    def two(w):
        def unit(p):
            fine_attend(w, p)
            fine_attend(w + 1, p)

        return unit

    staged.w_qkv_fine.wait()
    whole = [(0, SLOTS)]
    with_lon = [(0, KEPT), PARTS[1]]
    fine_rows(0, WINDOW, [(0, KEPT)])
    over_pairs(0, 4, 4, lambda p: fine_attend(0, p))
    tok[1].wait_recv()
    fine_rows(WINDOW, WINDOW, with_lon)
    over_pairs(0, 4, 4, lambda p: fine_attend(1, p))
    staged.w_out_fine.wait()
    fine_result(0, 2 * WINDOW)
    for i in (0, 2):
        off, size = PARTS[i]
        r.out_send[off - KEPT : off - KEPT + size] = fine_message(2 * WINDOW, PARTS[i])
    out = exchange(3, r.out_send, r.out_recv, PARTS, KEPT, down, (0, 2))
    tok[0].wait_recv()
    tok[2].wait_recv()
    top = exchange(2, r.top_send, r.top_recv, PARTS_C, KEPT_C, down)
    fine_rows(2 * WINDOW, 2 * WINDOW, whole)
    over_pairs(0, 4, 2, two(2))
    fine_result(2 * WINDOW, 2 * WINDOW)
    off, size = PARTS[1]
    r.out_send[off - KEPT : off - KEPT + size] = fine_message(CELLS, PARTS[1])
    out += exchange(3, r.out_send, r.out_recv, PARTS, KEPT, down, (1,))
    r.out_recv[:KEPT] = fine_message(CELLS, (0, KEPT))

    (normed,), _ = norm_parts([r.cells[...]])
    r.normed[0] = normed.astype(BF16)
    normed_swap = swap(r.normed.at[0], r.normed.at[1])
    mixed_swap = swap(r.mixed.at[0], r.mixed.at[1])
    staged.w_merge.wait()
    arrived(out)
    cot = exchange(1, r.cot_send, r.cot_recv, PARTS, KEPT, down)
    for k in range(4):
        r.merged[k] = dot(spread(TAKE_MERGE, WINDOW, SLOTS, k * WINDOW), r.out_recv[...])
    normed, _ = norm_parts([r.merged[k] for k in range(4)])
    coarse_in = jnp.zeros((WINDOW, COARSE), F32)
    for k in range(4):
        part = eighty(normed[k]).astype(BF16)
        r.normed_merge[0, :, k * WIDE : (k + 1) * WIDE] = part
        coarse_in += dot(
            normed[k].astype(BF16), r.v_w_merge[k * WIDE : (k + 1) * WIDE]
        )
    merge_swap = swap(r.normed_merge.at[0], r.normed_merge.at[1])
    r.coarse_in[...] = coarse_in.astype(BF16).astype(F32)
    (normed,), _ = norm_parts([r.coarse_in[...]])
    normed = normed.astype(BF16)
    staged.w_qkv_coarse.wait()
    for t in range(6):
        packed = dot(normed, r.v_w_qkv_coarse[:, t * WIDE : (t + 1) * WIDE])
        for p in range(4):
            r.packed_c[t % 2 * 4 + p, :, t // 2 * PAIR : (t // 2 + 1) * PAIR] = packed[
                :, p * PAIR : (p + 1) * PAIR
            ]
    staged.w_out_coarse.wait()
    take_coarse = spread(TAKE_COARSE, WINDOW, SLOTS_C)
    arrived(top)
    r.allowed_c[0] = allowed_of(dot(take_coarse, r.top_recv[:, COARSE:]))
    r.top[...] = dot(take_coarse, r.top_recv[:, :COARSE])
    for h in range(2):
        r.top_half[h] = eighty(r.top[:, h * WIDE : (h + 1) * WIDE]).astype(BF16)
    top_swap = swap(r.top_half.at[1 - core], r.top_other)
    over_pairs(0, 8, 4, lambda p: attend(
        r.packed_c, r.shares_c, r.attn_c, r.allowed_c, 0, p, 8
    ))
    for p in range(8):
        r.mixed_c[0, :, p * PAIR : (p + 1) * PAIR] = eighty(r.attn_c[p]).astype(BF16)
    mixed_c_swap = swap(r.mixed_c.at[0], r.mixed_c.at[1])

    grad_mixed = dot_nt(r.top[...].astype(BF16), r.v_w_out_coarse[...])
    for p in range(8):
        r.grad_mixed_c[p] = grad_mixed[:, p * PAIR : (p + 1) * PAIR].astype(BF16).astype(F32)

    def coarse_back(p):
        attend_back(r.packed_c, r.shares_c, r.grad_mixed_c, r.grad_packed_c, 0, p, 8)

    over_pairs(0, 4, 4, coarse_back)
    mixed_c_swap.wait_recv()
    top_swap.wait_recv()
    both = jnp.concatenate([r.top_half[core], r.top_other[...]], axis=0)
    for t in range(2):
        mixed = r.mixed_c[:, :, t * WIDE : (t + 1) * WIDE].reshape(160, WIDE)
        part = dot_tn(mixed, both).astype(BF16).reshape(8, 2, HALF_ROWS, WIDE)
        for g in range(2):
            put_blocks(out_c, g, t * 8, part[:, g])
    for part in out_c:
        part.start_first()
    over_pairs(4, 4, 4, coarse_back)
    grad_normed = jnp.zeros((WINDOW, COARSE), F32)
    for t in range(6):
        grads = jnp.concatenate(
            [
                r.grad_packed_c[t % 2 * 4 + p, :, t // 2 * PAIR : (t // 2 + 1) * PAIR]
                for p in range(4)
            ],
            axis=1,
        ).astype(BF16)
        grad_normed += dot_nt(grads, r.v_w_qkv_coarse[:, t * WIDE : (t + 1) * WIDE])
    normed, scale = norm_parts([r.coarse_in[...]])
    (back,) = norm_parts_back(normed, scale, [grad_normed])
    grad_coarse = r.top[...] + back
    for h in range(2):
        r.grad_coarse[h] = eighty(grad_coarse[:, h * WIDE : (h + 1) * WIDE]).astype(BF16)
    grad_coarse = grad_coarse.astype(BF16)
    coarse_swap = swap(r.grad_coarse.at[1 - core], r.grad_coarse_other)
    for k in range(4):
        r.grad_merged[k] = dot_nt(grad_coarse, r.v_w_merge[k * WIDE : (k + 1) * WIDE])
    normed, scale = norm_parts([r.merged[k] for k in range(4)])
    back = norm_parts_back(normed, scale, [r.grad_merged[k] for k in range(4)])
    back = jnp.concatenate(back, axis=0).astype(BF16)
    message = dot(spread(TAKE_MERGE_T, SLOTS, CELLS), back).astype(BF16)
    r.back_send[...] = message[KEPT:]
    r.back_recv[:KEPT] = message[:KEPT]
    back = exchange(4, r.back_send, r.back_recv, PARTS, KEPT, up)

    merge_swap.wait_recv()
    coarse_swap.wait_recv()
    both = jnp.concatenate([r.grad_coarse[core], r.grad_coarse_other[...]], axis=0)
    for k in range(4):
        normed = r.normed_merge[:, :, k * WIDE : (k + 1) * WIDE].reshape(160, WIDE)
        part = dot_tn(normed, both).astype(BF16).reshape(8, 2, HALF_ROWS, WIDE)
        for g in range(2):
            put_blocks(merge, g, k * 8, part[:, g])
    for part in merge:
        part.start_first()

    arrived(cot)
    r.grad_fine[...] = dot(spread(TAKE_WINDOWS, CELLS, SLOTS), r.cot_recv[...])

    def fine_rows_back(first, count, ranges):
        rows = slice(first, first + count)
        r.grad_fine[rows] += taken(
            SEND_WINDOWS_T, first, count, r.back_recv, ranges, slice(0, WIDE)
        )
        low = r.grad_fine[rows].astype(BF16)
        grad_mixed = dot_nt(low, r.v_w_out_fine[...])
        for p in range(4):
            r.attn[p, rows] = grad_mixed[:, p * PAIR : (p + 1) * PAIR].astype(BF16).astype(F32)

    def window_back(w, p):
        attend_back(r.packed, r.shares, r.attn, r.grad_packed, w, p, 4)

    fine_rows_back(3 * WINDOW, WINDOW, [(0, KEPT)])
    over_pairs(0, 4, 4, lambda p: window_back(3, p))
    back[1].wait_recv()
    fine_rows_back(2 * WINDOW, WINDOW, with_lon)
    over_pairs(0, 4, 4, lambda p: window_back(2, p))
    back[0].wait_recv()
    back[2].wait_recv()
    for part in out_c:
        part.start_second()
    fine_rows_back(0, 2 * WINDOW, whole)
    for h in range(2):
        r.grad_low[h] = r.grad_fine[:, h * 256 : (h + 1) * 256].astype(BF16)
    low_swap = swap(r.grad_low.at[1 - core], r.grad_low_other)

    def both_windows(p):
        window_back(0, p)
        window_back(1, p)

    other = 2 * (1 - core)
    over_pairs(other, 2, 2, both_windows)
    for i in range(2):
        r.grad_pair[other + i] = r.grad_packed[other + i].astype(BF16)
    pair_swap = swap(r.grad_pair.at[pl.ds(other, 2)], r.grad_pair_other)
    own = 2 * core
    over_pairs(own, 2, 2, both_windows)
    for i in range(2):
        r.grad_pair[own + i] = r.grad_packed[own + i].astype(BF16)
    mixed_swap.wait_recv()
    low_swap.wait_recv()
    both = jnp.concatenate([r.grad_low[core], r.grad_low_other[...]], axis=0)
    part = dot_tn(r.mixed[...].reshape(2 * CELLS, WIDE), both).astype(BF16)
    part = part.reshape(4, 4, HALF_ROWS, 256)
    for g in range(4):
        put_blocks(fine, g, 12, part[:, g])
    normed_swap.wait_recv()
    pair_swap.wait_recv()
    for i in range(2):
        both = jnp.concatenate([r.grad_pair[own + i], r.grad_pair_other[i]], axis=0)
        grads = dot_tn(r.normed[...].reshape(2 * CELLS, WIDE), both)
        for t in range(3):
            r.mixed_rows[i, pl.ds(t, WIDE, stride=3), :] = grads[:, t * PAIR : (t + 1) * PAIR]
    for b in range(12):
        rows = [
            jnp.concatenate(
                [r.mixed_rows[i, pl.ds(b * 128 + g * 32, 32), :] for i in range(2)], axis=1
            ).astype(BF16)
            for g in range(4)
        ]
        for g in range(4):
            put_blocks(fine, g, b, rows[g][None])
    for part in fine:
        part.start_first()
    grad_normed = jnp.zeros((CELLS, WIDE), F32)
    for t in range(3):
        grads = jnp.concatenate(
            [r.grad_pair[p, :, t * PAIR : (t + 1) * PAIR] for p in range(4)], axis=1
        )
        grad_normed += dot_nt(grads, r.v_w_qkv_fine[:, t * WIDE : (t + 1) * WIDE])
    normed, scale = norm_parts([r.cells[...]])
    (back_in,) = norm_parts_back(normed, scale, [grad_normed])
    grad_cells = (r.grad_fine[...] + back_in).astype(BF16)
    message = dot(spread(TAKE_WINDOWS_T, SLOTS, CELLS), grad_cells).astype(BF16)
    r.grad_send[...] = message[KEPT:]
    r.grad_recv[:KEPT] = message[:KEPT]
    grad = exchange(5, r.grad_send, r.grad_recv, PARTS, KEPT, up)
    for part in fine:
        part.start_second()
    for part in merge:
        part.start_second()
    arrived(grad)
    r.grad_tokens[...] = dot(
        spread(SEND_ROWS_T, CELLS, SLOTS), r.grad_recv[...]
    ).astype(BF16)
    for part in out_c + merge + fine:
        part.finish(r.total)

    total_swap = swap(r.total.at[1 - core], r.total_other)
    total_swap.wait_recv()
    here, there = r.total[core], r.total_other[...]
    halves = [jnp.where(core == 0, here, there), jnp.where(core == 0, there, here)]

    def out_fine():
        for h in range(2):
            for c in range(4):
                r.grad_flat[pl.ds(c // 2 * 128 + 2 * h + c % 2, 32, stride=4), :] = halves[h][
                    :, c * AUX : (c + 1) * AUX
                ]

    def out_coarse():
        for h in range(2):
            for c in range(4):
                r.grad_flat[pl.ds(4 * h + c, 32, stride=8), :] = halves[h][
                    :, c * AUX : (c + 1) * AUX
                ]

    when(me.lat < 2, out_fine)
    when(me.lat >= 2, out_coarse)
    for part in out_c + merge + fine:
        part.drain()
    for copies in (tok, cot, top, out, back, grad, swaps):
        for copy in copies:
            copy.wait_send()


def per_device(n_lat, n_lon, tokens, cot_fine, cot_coarse, mask_ids, pad_flags,
               w_qkv_fine, w_out_fine, w_merge, w_qkv_coarse, w_out_coarse):
    given = dict(
        maps=jnp.asarray(index_maps()),
        tokens=tokens.reshape(CELLS, WIDE),
        cot_fine=cot_fine.reshape(CELLS, WIDE),
        cot_coarse=cot_coarse.reshape(cot_coarse.shape[1:]),
        w_qkv_fine=w_qkv_fine, w_out_fine=w_out_fine, w_merge=w_merge,
        w_qkv_coarse=w_qkv_coarse, w_out_coarse=w_out_coarse,
    )
    small = dict(
        mask_ids=mask_ids.reshape(ROWS, 1, COLS), pad_flags=pad_flags.reshape(ROWS, 1, COLS)
    )
    outs = dict(
        grad_tokens=((CELLS, WIDE), BF16),
        grad_flat=((256, AUX), F32),
    )
    scratch = {"v_" + name: (given[name].shape, given[name].dtype) for name in given}
    scratch.update(
        tok_send=((SLOTS - KEPT, WIDE + AUX), BF16),
        tok_recv=((SLOTS, WIDE + AUX), BF16),
        cot_send=((SLOTS - KEPT, WIDE), BF16),
        cot_recv=((SLOTS, WIDE), BF16),
        top_send=((SLOTS_C - KEPT_C, COARSE + AUX), BF16),
        top_recv=((SLOTS_C, COARSE + AUX), BF16),
        out_send=((SLOTS - KEPT, WIDE), BF16),
        out_recv=((SLOTS, WIDE), BF16),
        back_send=((SLOTS - KEPT, WIDE), BF16),
        back_recv=((SLOTS, WIDE), BF16),
        grad_send=((SLOTS - KEPT, WIDE), BF16),
        grad_recv=((SLOTS, WIDE), BF16),
        allowed=((4, 2 * WINDOW, WINDOW), F32),
        allowed_c=((1, 2 * WINDOW, WINDOW), F32),
        cells=((CELLS, WIDE), F32),
        fine_out=((CELLS, WIDE), BF16),
        normed=((2, CELLS, WIDE), BF16),
        packed=((4, CELLS, 3 * PAIR), F32),
        shares=((16, 2 * WINDOW, WINDOW), F32),
        attn=((4, CELLS, PAIR), F32),
        mixed=((2, CELLS, WIDE), BF16),
        top=((WINDOW, COARSE), F32),
        top_half=((2, 80, WIDE), BF16),
        top_other=((80, WIDE), BF16),
        grad_mixed_c=((8, WINDOW, PAIR), F32),
        merged=((4, WINDOW, WIDE), F32),
        normed_merge=((2, 80, 4 * WIDE), BF16),
        grad_merged=((4, WINDOW, WIDE), F32),
        coarse_in=((WINDOW, COARSE), F32),
        packed_c=((8, WINDOW, 3 * PAIR), F32),
        shares_c=((8, 2 * WINDOW, WINDOW), F32),
        attn_c=((8, WINDOW, PAIR), F32),
        mixed_c=((2, 80, COARSE), BF16),
        grad_packed_c=((8, WINDOW, 3 * PAIR), F32),
        grad_coarse=((2, 80, WIDE), BF16),
        grad_coarse_other=((80, WIDE), BF16),
        grad_fine=((CELLS, WIDE), F32),
        grad_low=((2, CELLS, 256), BF16),
        grad_low_other=((CELLS, 256), BF16),
        grad_packed=((4, CELLS, 3 * PAIR), F32),
        grad_pair=((4, CELLS, 3 * PAIR), BF16),
        grad_pair_other=((2, CELLS, 3 * PAIR), BF16),
        mixed_rows=((2, 3 * WIDE, AUX), F32),
        total=((2, HALF_ROWS, WIDE), F32),
        total_other=((HALF_ROWS, WIDE), F32),
    )
    sems = dict(
        stage_sem=len(given), send_sem=18, recv_sem=18, swap_send=16, swap_recv=16
    )
    for name, (_, lats, parts) in SEGMENTS.items():
        for axis, (_, cols) in parts.items():
            kept = kept_shape(lats, axis)
            block = (HALF_ROWS, cols)
            scratch["pa_" + name + axis] = ((lats, 4, 2) + block, BF16)
            scratch["ri_" + name + axis] = ((3,) + kept + block, BF16)
            scratch["la_" + name + axis] = (kept + block, BF16)
            scratch["fi_" + name + axis] = ((16,) + block, BF16)
            sems["s1_" + name + axis] = sems["r1_" + name + axis] = 3
            sems["s2_" + name + axis], sems["r2_" + name + axis] = 8, 16
    names = (
        ["in_" + name for name in given] + list(small)
        + list(outs) + list(scratch) + list(sems)
    )

    def kernel(*refs):
        body(n_lat, n_lon, list(given), names, refs)

    vmem = pl.BlockSpec(memory_space=pltpu.VMEM)
    results = pl.pallas_call(
        kernel,
        out_shape=[jax.ShapeDtypeStruct(*s) for s in outs.values()],
        in_specs=[pl.BlockSpec(memory_space=pl.ANY)] * len(given) + [vmem, vmem],
        out_specs=[vmem] * len(outs),
        scratch_shapes=[pltpu.VMEM(*s) for s in scratch.values()]
        + [pltpu.SemaphoreType.DMA((n,)) for n in sems.values()],
        compiler_params=pltpu.CompilerParams(
            collective_id=0, has_side_effects=True, vmem_limit_bytes=60 * 2**20
        ),
        name="swin_backward",
    )(*[given[name] for name in given], *small.values())
    return results[0].reshape(tokens.shape), results[1].reshape(-1)


def solution(mesh):
    cells = P(None, "lat", "lon", None)
    ids = P(None, "lat", "lon")
    step = functools.partial(per_device, mesh.shape["lat"], mesh.shape["lon"])
    return jax.shard_map(
        step,
        mesh=mesh,
        in_specs=(cells, cells, cells, ids, ids) + (P(),) * 5,
        out_specs=(cells, P(("lat", "lon"))),
        check_vma=False,
    )
```

```python
import functools
import types

import jax
import jax.numpy as jnp
import numpy as np
from jax import lax
from jax.experimental import pallas as pl
from jax.experimental.pallas import tpu as pltpu
from jax.sharding import PartitionSpec as P

WIN_LAT = 6
WIN_LON = 12
ROWS = 12
COLS = 24
CELLS = ROWS * COLS
WINDOW = WIN_LAT * WIN_LON
WIDE = 512
COARSE = 1024
HEAD = 64
PAIR = 2 * HEAD
AUX = 128
MESH = pl.DeviceIdType.MESH
F32 = jnp.float32
BF16 = jnp.bfloat16

KEPT = 176
PARTS = ((176, 64), (240, 64), (304, 32))
SLOTS = 336
KEPT_C = 32
PARTS_C = ((32, 32), (64, 32), (96, 32))
SLOTS_C = 128


def slot_of(a, b, half_lat, half_lon, cols, offsets):
    if a >= half_lat and b >= half_lon:
        return (a - half_lat) * (cols - half_lon) + b - half_lon
    if b >= half_lon:
        return offsets[0] + a * (cols - half_lon) + b - half_lon
    if a >= half_lat:
        return offsets[1] + (a - half_lat) * half_lon + b
    return offsets[2] + a * half_lon + b


(
    SEND_ROWS, TAKE_WINDOWS, SEND_WINDOWS, TAKE_MERGE,
    SEND_ROWS_T, TAKE_WINDOWS_T, SEND_WINDOWS_T, TAKE_MERGE_T,
    SEND_COARSE, TAKE_COARSE, SEND_IDS, ROW_OF, COL_OF,
) = range(13)


def index_maps():
    fine = [off for off, _ in PARTS]
    coarse = [off for off, _ in PARTS_C]
    table = np.full((SLOTS, AUX), -1, np.int32)
    for a in range(ROWS):
        for b in range(COLS):
            cell = a * COLS + b
            here = slot_of(a, b, 3, 6, COLS, fine)
            came = slot_of((a + 3) % ROWS, (b + 6) % COLS, 3, 6, COLS, fine)
            window = (a // 6 * 2 + b // 12) * WINDOW + a % 6 * 12 + b % 12
            quarter = (a % 2 * 2 + b % 2) * WINDOW + a // 2 * 12 + b // 2
            for name, row, source in (
                (SEND_ROWS, here, cell),
                (TAKE_WINDOWS, window, came),
                (SEND_WINDOWS, here, window),
                (TAKE_MERGE, quarter, came),
            ):
                table[row, name] = source
                table[source, name + SEND_ROWS_T] = row
            table[cell, ROW_OF] = a
            table[cell, COL_OF] = b
    for i in range(6):
        for j in range(12):
            here = slot_of(i, j, 3, 6, 12, coarse)
            came = slot_of((i + 3) % 6, (j + 6) % 12, 3, 6, 12, coarse)
            table[here, SEND_COARSE] = i * 12 + j
            table[i * 12 + j, TAKE_COARSE] = came
            table[here, SEND_IDS] = 2 * i * COLS + 2 * j
    return table


def dot(a, b):
    return jnp.dot(a, b, preferred_element_type=F32)


def dot_nt(a, b):
    return lax.dot_general(a, b, (((1,), (1,)), ((), ())), preferred_element_type=F32)


def dot_tn(a, b):
    return lax.dot_general(a, b, (((0,), (0,)), ((), ())), preferred_element_type=F32)


def norm_parts(parts):
    size = sum(p.shape[-1] for p in parts)
    average = sum(jnp.sum(p, axis=-1, keepdims=True) for p in parts) * (1.0 / size)
    centred = [p - average for p in parts]
    spread = sum(jnp.sum(c * c, axis=-1, keepdims=True) for c in centred) * (1.0 / size)
    scale = lax.rsqrt(spread + 1e-05)
    return [c * scale for c in centred], scale


def norm_parts_back(normed, scale, grads):
    size = sum(p.shape[-1] for p in normed)
    flat = sum(jnp.sum(g, axis=-1, keepdims=True) for g in grads) * (1.0 / size)
    along = sum(
        jnp.sum(g * n, axis=-1, keepdims=True) for g, n in zip(grads, normed)
    ) * (1.0 / size)
    return [scale * (g - flat - n * along) for g, n in zip(grads, normed)]


def first_lanes():
    return lax.broadcasted_iota(jnp.int32, (WINDOW, PAIR), 1) < HEAD


def stacked(x, low):
    return jnp.concatenate([jnp.where(low, x, 0.0), jnp.where(low, 0.0, x)], axis=0)


def split_bf16(x):
    high = x.astype(BF16)
    return high, (x - high.astype(F32)).astype(BF16)


def allowed_of(ids):
    pick = (lax.broadcasted_iota(jnp.int32, (8, AUX), 1) == 0).astype(BF16)
    along = dot_nt(pick, ids.astype(BF16))[0:1]
    same = jnp.where(ids[:, 0:1] == along, 1.0, 0.0)
    return jnp.concatenate([same, same], axis=0)


def pair_forward(q, k, v, allowed, low):
    q_high, q_low = split_bf16(stacked(q * HEAD**-0.5, low))
    k_high, k_low = split_bf16(k)
    scores = dot_nt(
        jnp.concatenate([q_high, q_low], axis=1), jnp.concatenate([k_high, k_high], axis=1)
    ) + dot_nt(q_high, k_low)
    scores = jnp.where(allowed > 0.0, scores, -1e30)
    weights = jnp.exp(scores - jnp.max(scores, axis=-1, keepdims=True)).astype(BF16)
    result = dot(weights, jnp.concatenate([v.astype(BF16), jnp.ones_like(v, BF16)], axis=1))
    scale = 1.0 / result[:, PAIR:]
    result = result[:, :PAIR] * scale
    shares = weights.astype(F32) * scale[:, :WINDOW]
    return shares.T, jnp.where(low, result[:WINDOW], result[WINDOW:])


def pair_backward(q, k, v, shares, grad, low):
    grad2 = stacked(grad, low).astype(BF16)
    q2 = stacked(q, low).astype(BF16)
    grad_shares = dot_nt(v.astype(BF16), grad2)
    delta = jnp.sum(grad_shares * shares, axis=0, keepdims=True)
    grad_scores = (shares * (grad_shares - delta) * HEAD**-0.5).astype(BF16)
    grad_q = dot_tn(grad_scores, k.astype(BF16))
    grad_q = jnp.where(low, grad_q[:WINDOW], grad_q[WINDOW:])
    return grad_q, dot(grad_scores, q2), dot(shares.astype(BF16), grad2)


def attend(packed, shares, attn, allowed, w, p, pairs):
    rows = slice(w * WINDOW, (w + 1) * WINDOW)
    low = first_lanes()
    q, k, v = (packed[p, rows, t * PAIR : (t + 1) * PAIR] for t in range(3))
    part, result = pair_forward(q, k, v, allowed[w], low)
    shares[w * pairs + p] = part
    attn[p, rows] = result


def attend_back(packed, shares, grad, grad_packed, w, p, pairs):
    rows = slice(w * WINDOW, (w + 1) * WINDOW)
    low = first_lanes()
    q, k, v = (packed[p, rows, t * PAIR : (t + 1) * PAIR] for t in range(3))
    grads = pair_backward(q, k, v, shares[w * pairs + p], grad[p, rows], low)
    for t in range(3):
        grad_packed[p, rows, t * PAIR : (t + 1) * PAIR] = grads[t]


def over_pairs(first, pairs, step, unit):
    def some(n, carry):
        for i in range(step):
            unit(first + n * step + i)
        return carry

    lax.fori_loop(0, pairs // step, some, 0)


SEGMENTS = dict(
    out_c=(6, 2, dict(z=(0, 512), y=(512, 256), x=(768, 256))),
    merge=(2, 4, dict(z=(0, 384), y=(384, 384), x=(768, 256))),
    fine0=(0, 2, dict(z=(0, 256), y=(256, 128), x=(384, 128))),
    fine1=(0, 2, dict(z=(0, 256), y=(256, 128), x=(384, 128))),
)
HALF_ROWS = 32


class Place:
    def __init__(self, lat, lon):
        self.lat, self.y, self.x_high = lat, lat % 4, lat // 4
        self.z, self.x_low, self.core = lon // 4, lon // 2 % 2, lon % 2
        self.x = self.x_high * 2 + self.x_low

    def chip(self, x, y, z):
        return (x // 2 * 4 + y, z * 4 + x % 2 * 2 + self.core)

    def shifted(self, dx, dy, dz):
        return self.chip(
            lax.rem(self.x + dx, 4), lax.rem(self.y + dy, 4), lax.rem(self.z + dz, 4)
        )

    def sibling(self):
        return (self.lat, self.z * 4 + self.x_low * 2 + 1 - self.core)


def remote(src, dst, send_sem, recv_sem, peer):
    return pltpu.make_async_remote_copy(
        src_ref=src, dst_ref=dst, send_sem=send_sem, recv_sem=recv_sem,
        device_id=peer, device_id_type=MESH,
    )


class Part:
    def __init__(self, r, name, axis, me):
        self.first, self.lats, parts = SEGMENTS[name]
        self.left, self.cols = parts[axis]
        self.axis, self.me, self.all = axis, me, self.lats == 4
        (self.part, self.ring, self.last, self.final, self.send, self.recv, self.send2,
         self.recv2) = (
            getattr(r, what + name + axis)
            for what in ("pa_", "ri_", "la_", "fi_", "s1_", "r1_", "s2_", "r2_")
        )
        self.kept = kept_shape(self.lats, axis)
        self.ring2, self.mid, self.send3, self.recv3 = (
            getattr(r, what + name + axis) for what in ("r2i_", "mid_", "s3_", "r3_")
        )
        self.axis2 = {"z": "y", "y": "z", "x": "z"}[axis]
        self.axis3 = {"z": "x", "y": "x", "x": "y"}[axis]
        self.number3 = {"x": me.x, "y": me.y}[self.axis3]
        self.holds = True
        if not self.all and axis != "z":
            self.holds = self.among(me.y if axis == "y" else me.x)
        self.holds2 = self.holds
        if not self.all and axis == "z":
            self.holds2 = self.among(me.y)
        self.owns = jnp.logical_and(me.lat >= self.first, me.lat < self.first + self.lats)

    def among(self, index):
        return index // 2 == self.first // 4

    def source(self, to):
        if self.axis == "z":
            return self.part.at[:, to], True
        if self.axis == "x":
            if self.all:
                return self.part.at[pl.ds(to // 2 * 2, 2), :, to % 2], True
            return self.part.at[:, :, to % 2], self.among(to)
        if self.all:
            return self.part.at[lax.rem(to + 2, 4)], True
        return self.part.at[to % 2], self.among(to)

    def mine(self, i, j):
        me = self.me
        if self.axis == "z":
            return self.part[i, me.z, j]
        if self.axis == "x":
            return self.part[(me.x_high * 2 if self.all else 0) + i, j, me.x_low]
        return self.part[lax.rem(me.y + 2, 4) if self.all else me.y % 2, i, j]

    def firsts(self):
        me = self.me
        here = {"x": me.x, "y": me.y, "z": me.z}[self.axis]
        for d in range(1, 4):
            src, some = self.source(lax.rem(here + d, 4))
            shift = [d if self.axis == a else 0 for a in "xyz"]
            yield some, remote(
                src, self.ring.at[d - 1], self.send.at[d - 1], self.recv.at[d - 1],
                me.shifted(*shift),
            )

    def thirds(self):
        me = self.me
        for i in range(2):
            if self.axis3 == "x":
                to = ((1 - me.y // 2) if self.all else self.first // 4) * 2 + i
                peer = me.chip(to, me.y, me.z)
            else:
                to = 2 * ((1 - me.x_high) if self.all else self.first // 4) + i
                peer = me.chip(me.x, to, me.z)
            yield both(self.holds2, to != self.number3), remote(
                self.mid.at[i], self.final.at[self.number3], self.send3.at[i],
                self.recv3.at[self.number3], peer,
            )

    def seconds(self):
        me = self.me
        here = {"y": me.y, "z": me.z}[self.axis2]
        for d in range(1, 4):
            to = lax.rem(here + d, 4)
            going = self.holds
            src = {"z": lax.rem(to + 2, 4), "y": to, "x": (slice(None), to)}[self.axis]
            if self.axis == "z" and not self.all:
                src, going = to % 2, both(going, self.among(to))
            shift = [d if self.axis2 == a else 0 for a in "xyz"]
            yield going, remote(
                self.last.at[src], self.ring2.at[d - 1], self.send2.at[d - 1],
                self.recv2.at[d - 1], me.shifted(*shift),
            )

    def start_third(self):
        me = self.me

        def add():
            for _, copy in self.seconds():
                copy.wait_recv()
            for i in range(2):
                own = {
                    "z": (lax.rem(me.y + 2, 4) if self.all else me.y % 2, i),
                    "y": (me.z, i), "x": (i, me.z),
                }[self.axis]
                total = self.last[own].astype(F32)
                for d in range(3):
                    total += self.ring2[d, i].astype(F32)
                self.mid[i] = total.astype(BF16)

        when(self.holds2, add)
        for going, copy in self.thirds():
            when(going, copy.start)

    def start_first(self):
        for some, copy in self.firsts():
            when(some, copy.start)

    def start_second(self):
        def add():
            for _, copy in self.firsts():
                copy.wait_recv()
            for i in range(self.kept[0]):
                for j in range(self.kept[1]):
                    total = self.mine(i, j).astype(F32)
                    for d in range(3):
                        total += self.ring[d, i, j].astype(F32)
                    self.last[i, j] = total.astype(BF16)

        when(self.holds, add)
        for going, copy in self.seconds():
            when(going, copy.start)

    def finish(self, total):
        me = self.me

        def add():
            for n in range(4):
                copy = remote(
                    self.mid.at[0], self.final.at[n], self.send3.at[0], self.recv3.at[n],
                    me.sibling(),
                )
                when(self.number3 != n, copy.wait_recv)
            self.final[self.number3] = self.mid[me.x_low if self.axis3 == "x" else me.y % 2]
            for c in range(0, self.cols, AUX):
                value = self.final[0, :, c : c + AUX].astype(F32)
                for n in range(1, 4):
                    value += self.final[n, :, c : c + AUX].astype(F32)
                at = self.left + c
                half = total.shape[-1]
                total[at // half, :, at % half : at % half + AUX] = value

        when(self.owns, add)

    def drain(self):
        for some, copy in self.firsts():
            when(some, copy.wait_send)
        for going, copy in self.seconds():
            when(going, copy.wait_send)
        for going, copy in self.thirds():
            when(going, copy.wait_send)


def both(one, other):
    return other if one is True else one if other is True else jnp.logical_and(one, other)


def when(condition, step):
    if condition is True:
        step()
    else:
        pl.when(condition)(step)


def kept_shape(lats, axis):
    return {"z": (lats, 2), "x": (2, 4), "y": (4, 2)}[axis]


def put_blocks(parts, group, first, value):
    size = value.shape[-1]
    for part in parts:
        low = max(group * size, part.left)
        high = min((group + 1) * size, part.left + part.cols)
        if low < high:
            for b in range(value.shape[0]):
                n = first + b
                part.part[n // 8, n // 2 % 4, n % 2, :, low - part.left : high - part.left] = (
                    value[b, :, low - group * size : high - group * size]
                )


def eighty(x):
    return jnp.concatenate([x, jnp.zeros((80 - x.shape[0], x.shape[1]), x.dtype)], axis=0)


def body(n_lat, n_lon, given, names, refs):
    r = types.SimpleNamespace(**dict(zip(names, refs)))
    lat, lon = lax.axis_index("lat"), lax.axis_index("lon")
    lat_up, lat_down = lax.rem(lat + 1, n_lat), lax.rem(lat + n_lat - 1, n_lat)
    lon_up, lon_down = lax.rem(lon + 1, n_lon), lax.rem(lon + n_lon - 1, n_lon)
    down = ((lat_down, lon), (lat, lon_down), (lat_down, lon_down))
    up = ((lat_up, lon), (lat, lon_up), (lat_up, lon_up))

    staged = types.SimpleNamespace()
    for i, name in enumerate(given):
        copy = pltpu.make_async_copy(
            getattr(r, "in_" + name), getattr(r, "v_" + name), r.stage_sem.at[i]
        )
        setattr(staged, name, copy)
        copy.start()

    barrier = pltpu.get_barrier_semaphore()
    me = Place(lat, lon)
    core = me.core
    peers = [down[1], down[2], up[1], up[2]]
    for a in range(4):
        for b in range(4):
            peers += [me.shifted(a, b, 0)] if a or b else []
        peers += [me.shifted(0, 0, a)] if a else []
    for peer in peers:
        pl.semaphore_signal(barrier, inc=1, device_id=peer, device_id_type=MESH)

    sums = {
        name: [Part(r, name, axis, me) for axis in parts]
        for name, (_, _, parts) in SEGMENTS.items()
    }
    out_c, merge, *fine = sums.values()

    def exchange(turn, src, dst, parts, kept, peers, which=(0, 1, 2)):
        copies = []
        for i in which:
            off, size = parts[i]
            copies.append(
                remote(
                    src.at[pl.ds(off - kept, size)], dst.at[pl.ds(off, size)],
                    r.send_sem.at[3 * turn + i], r.recv_sem.at[3 * turn + i], peers[i],
                )
            )
            copies[-1].start()
        return copies

    def arrived(copies):
        for copy in copies:
            copy.wait_recv()

    swaps = []

    def swap(src, dst):
        n = len(swaps)
        swaps.append(remote(src, dst, r.swap_send.at[n], r.swap_recv.at[n], me.sibling()))
        swaps[-1].start()
        return swaps[-1]

    def one_hot(name, rows, cols, first=0, base=0):
        wanted = r.v_maps[first : first + rows, name : name + 1] - base
        place = lax.broadcasted_iota(jnp.int32, (rows, cols), 1)
        return jnp.where(place == wanted, 1.0, 0.0)

    def spread(name, rows, cols, first=0, base=0):
        return one_hot(name, rows, cols, first, base).astype(BF16)

    staged.maps.wait()
    staged.tokens.wait()
    send_rows = spread(SEND_ROWS, SLOTS, CELLS)
    mask = r.mask_ids[:, 0, :].astype(F32).astype(BF16)
    flags = r.pad_flags[:, 0, :].astype(F32).astype(BF16)
    row_of, col_of = spread(ROW_OF, CELLS, ROWS), one_hot(COL_OF, CELLS, COLS)
    ids = jnp.sum(dot(row_of, mask) * col_of, axis=-1, keepdims=True)
    flag_rows = jnp.sum(dot(row_of, flags) * col_of, axis=-1, keepdims=True)
    aux = jnp.where(
        lax.broadcasted_iota(jnp.int32, (CELLS, AUX), 1) == 0, ids, 0.0
    ).astype(BF16)
    message = dot(send_rows, r.v_tokens[...]).astype(BF16)
    r.tok_send[:, :WIDE] = message[KEPT:]
    r.tok_recv[:KEPT, :WIDE] = message[:KEPT]
    message = dot(send_rows, aux).astype(BF16)
    r.tok_send[:, WIDE:] = message[KEPT:]
    r.tok_recv[:KEPT, WIDE:] = message[:KEPT]
    pl.semaphore_wait(barrier, len(peers))
    tok = exchange(0, r.tok_send, r.tok_recv, PARTS, KEPT, down)
    staged.cot_fine.wait()
    flagged = (r.v_cot_fine[...].astype(F32) * flag_rows).astype(BF16)
    message = dot(send_rows, flagged).astype(BF16)
    r.cot_send[...] = message[KEPT:]
    r.cot_recv[:KEPT] = message[:KEPT]
    staged.cot_coarse.wait()
    message = jnp.zeros((SLOTS_C, COARSE), F32)
    for i in range(6):
        message += dot(spread(SEND_COARSE, SLOTS_C, 12, 0, 12 * i), r.v_cot_coarse[i])
    message = message.astype(BF16)
    r.top_send[:, :COARSE] = message[KEPT_C:]
    r.top_recv[:KEPT_C, :COARSE] = message[:KEPT_C]
    message = dot(spread(SEND_IDS, SLOTS_C, CELLS), aux).astype(BF16)
    r.top_send[:, COARSE:] = message[KEPT_C:]
    r.top_recv[:KEPT_C, COARSE:] = message[:KEPT_C]

    def taken(name, first, count, source, ranges, cols):
        return sum(
            dot(spread(name, count, size, first, off), source[off : off + size, cols])
            for off, size in ranges
        )

    def fine_rows(first, count, ranges):
        rows = slice(first, first + count)
        ids = taken(TAKE_WINDOWS, first, count, r.tok_recv, ranges, slice(WIDE, WIDE + AUX))
        for w in range(count // WINDOW):
            r.allowed[first // WINDOW + w] = allowed_of(ids[w * WINDOW : (w + 1) * WINDOW])
        r.cells[rows] = taken(
            TAKE_WINDOWS, first, count, r.tok_recv, ranges, slice(0, WIDE)
        )
        (normed,), _ = norm_parts([r.cells[rows]])
        normed = normed.astype(BF16)
        for t in range(3):
            packed = dot(normed, r.v_w_qkv_fine[:, t * WIDE : (t + 1) * WIDE])
            for p in range(4):
                r.packed[p, rows, t * PAIR : (t + 1) * PAIR] = packed[
                    :, p * PAIR : (p + 1) * PAIR
                ]

    def fine_attend(w, p):
        attend(r.packed, r.shares, r.attn, r.allowed, w, p, 4)

    def fine_result(first, count):
        rows = slice(first, first + count)
        mixed = jnp.concatenate([r.attn[p, rows] for p in range(4)], axis=1).astype(BF16)
        r.mixed[0, rows] = mixed
        fine_out = r.cells[rows] + dot(mixed, r.v_w_out_fine[...])
        r.fine_out[rows] = fine_out.astype(BF16)

    def fine_message(rows, slots):
        first, size = slots
        return dot(spread(SEND_WINDOWS, size, rows, first), r.fine_out[:rows]).astype(BF16)

    staged.w_qkv_fine.wait()
    whole = [(0, SLOTS)]
    with_lon = [(0, KEPT), PARTS[1]]
    fine_rows(0, WINDOW, [(0, KEPT)])
    over_pairs(0, 4, 4, lambda p: fine_attend(0, p))
    tok[1].wait_recv()
    fine_rows(WINDOW, WINDOW, with_lon)
    over_pairs(0, 4, 4, lambda p: fine_attend(1, p))
    staged.w_out_fine.wait()
    fine_result(0, 2 * WINDOW)
    for i in (0, 2):
        off, size = PARTS[i]
        r.out_send[off - KEPT : off - KEPT + size] = fine_message(2 * WINDOW, PARTS[i])
    out = exchange(3, r.out_send, r.out_recv, PARTS, KEPT, down, (0, 2))
    tok[0].wait_recv()
    tok[2].wait_recv()
    top = exchange(2, r.top_send, r.top_recv, PARTS_C, KEPT_C, down)
    fine_rows(2 * WINDOW, 2 * WINDOW, whole)
    over_pairs(0, 4, 4, lambda p: fine_attend(2, p))
    fine_result(2 * WINDOW, WINDOW)
    off, size = PARTS[1]
    r.out_send[off - KEPT : off - KEPT + size] = fine_message(3 * WINDOW, PARTS[1])
    out += exchange(3, r.out_send, r.out_recv, PARTS, KEPT, down, (1,))
    over_pairs(0, 4, 4, lambda p: fine_attend(3, p))
    fine_result(3 * WINDOW, WINDOW)
    r.out_recv[:KEPT] = fine_message(CELLS, (0, KEPT))

    (normed,), _ = norm_parts([r.cells[...]])
    r.normed[0] = normed.astype(BF16)
    normed_swap = swap(r.normed.at[0], r.normed.at[1])
    mixed_swap = swap(r.mixed.at[0], r.mixed.at[1])
    staged.w_merge.wait()
    arrived(out)
    cot = exchange(1, r.cot_send, r.cot_recv, PARTS, KEPT, down)
    for k in range(4):
        r.merged[k] = dot(spread(TAKE_MERGE, WINDOW, SLOTS, k * WINDOW), r.out_recv[...])
    normed, _ = norm_parts([r.merged[k] for k in range(4)])
    coarse_in = jnp.zeros((WINDOW, COARSE), F32)
    for k in range(4):
        part = eighty(normed[k]).astype(BF16)
        r.normed_merge[0, :, k * WIDE : (k + 1) * WIDE] = part
        coarse_in += dot(
            normed[k].astype(BF16), r.v_w_merge[k * WIDE : (k + 1) * WIDE]
        )
    merge_swap = swap(r.normed_merge.at[0], r.normed_merge.at[1])
    r.coarse_in[...] = coarse_in.astype(BF16).astype(F32)
    (normed,), _ = norm_parts([r.coarse_in[...]])
    normed = normed.astype(BF16)
    staged.w_qkv_coarse.wait()
    for t in range(6):
        packed = dot(normed, r.v_w_qkv_coarse[:, t * WIDE : (t + 1) * WIDE])
        for p in range(4):
            r.packed_c[t % 2 * 4 + p, :, t // 2 * PAIR : (t // 2 + 1) * PAIR] = packed[
                :, p * PAIR : (p + 1) * PAIR
            ]
    staged.w_out_coarse.wait()
    take_coarse = spread(TAKE_COARSE, WINDOW, SLOTS_C)
    arrived(top)
    r.allowed_c[0] = allowed_of(dot(take_coarse, r.top_recv[:, COARSE:]))
    r.top[...] = dot(take_coarse, r.top_recv[:, :COARSE])
    for h in range(2):
        r.top_half[h] = eighty(r.top[:, h * WIDE : (h + 1) * WIDE]).astype(BF16)
    top_swap = swap(r.top_half.at[1 - core], r.top_other)
    over_pairs(0, 8, 4, lambda p: attend(
        r.packed_c, r.shares_c, r.attn_c, r.allowed_c, 0, p, 8
    ))
    for p in range(8):
        r.mixed_c[0, :, p * PAIR : (p + 1) * PAIR] = eighty(r.attn_c[p]).astype(BF16)
    mixed_c_swap = swap(r.mixed_c.at[0], r.mixed_c.at[1])

    grad_mixed = dot_nt(r.top[...].astype(BF16), r.v_w_out_coarse[...])
    for p in range(8):
        r.grad_mixed_c[p] = grad_mixed[:, p * PAIR : (p + 1) * PAIR].astype(BF16).astype(F32)

    def coarse_back(p):
        attend_back(r.packed_c, r.shares_c, r.grad_mixed_c, r.grad_packed_c, 0, p, 8)

    over_pairs(0, 4, 4, coarse_back)
    mixed_c_swap.wait_recv()
    top_swap.wait_recv()
    both = jnp.concatenate([r.top_half[core], r.top_other[...]], axis=0)
    for t in range(2):
        mixed = r.mixed_c[:, :, t * WIDE : (t + 1) * WIDE].reshape(160, WIDE)
        part = dot_tn(mixed, both).astype(BF16).reshape(8, 2, HALF_ROWS, WIDE)
        for g in range(2):
            put_blocks(out_c, g, t * 8, part[:, g])
    for part in out_c:
        part.start_first()
    over_pairs(4, 4, 4, coarse_back)
    grad_normed = jnp.zeros((WINDOW, COARSE), F32)
    for t in range(6):
        grads = jnp.concatenate(
            [
                r.grad_packed_c[t % 2 * 4 + p, :, t // 2 * PAIR : (t // 2 + 1) * PAIR]
                for p in range(4)
            ],
            axis=1,
        ).astype(BF16)
        grad_normed += dot_nt(grads, r.v_w_qkv_coarse[:, t * WIDE : (t + 1) * WIDE])
    normed, scale = norm_parts([r.coarse_in[...]])
    (back,) = norm_parts_back(normed, scale, [grad_normed])
    grad_coarse = r.top[...] + back
    for h in range(2):
        r.grad_coarse[h] = eighty(grad_coarse[:, h * WIDE : (h + 1) * WIDE]).astype(BF16)
    grad_coarse = grad_coarse.astype(BF16)
    coarse_swap = swap(r.grad_coarse.at[1 - core], r.grad_coarse_other)
    for k in range(4):
        r.grad_merged[k] = dot_nt(grad_coarse, r.v_w_merge[k * WIDE : (k + 1) * WIDE])
    normed, scale = norm_parts([r.merged[k] for k in range(4)])
    back = norm_parts_back(normed, scale, [r.grad_merged[k] for k in range(4)])
    back = jnp.concatenate(back, axis=0).astype(BF16)
    message = dot(spread(TAKE_MERGE_T, SLOTS, CELLS), back).astype(BF16)
    r.back_send[...] = message[KEPT:]
    r.back_recv[:KEPT] = message[:KEPT]
    back = exchange(4, r.back_send, r.back_recv, PARTS, KEPT, up)

    merge_swap.wait_recv()
    coarse_swap.wait_recv()
    both = jnp.concatenate([r.grad_coarse[core], r.grad_coarse_other[...]], axis=0)
    for k in range(4):
        normed = r.normed_merge[:, :, k * WIDE : (k + 1) * WIDE].reshape(160, WIDE)
        part = dot_tn(normed, both).astype(BF16).reshape(8, 2, HALF_ROWS, WIDE)
        for g in range(2):
            put_blocks(merge, g, k * 8, part[:, g])
    for part in merge:
        part.start_first()

    arrived(cot)
    r.grad_fine[...] = dot(spread(TAKE_WINDOWS, CELLS, SLOTS), r.cot_recv[...])

    def fine_rows_back(first, count, ranges):
        rows = slice(first, first + count)
        r.grad_fine[rows] += taken(
            SEND_WINDOWS_T, first, count, r.back_recv, ranges, slice(0, WIDE)
        )
        low = r.grad_fine[rows].astype(BF16)
        grad_mixed = dot_nt(low, r.v_w_out_fine[...])
        for p in range(4):
            r.attn[p, rows] = grad_mixed[:, p * PAIR : (p + 1) * PAIR].astype(BF16).astype(F32)

    def window_back(w, p):
        attend_back(r.packed, r.shares, r.attn, r.grad_packed, w, p, 4)

    fine_rows_back(3 * WINDOW, WINDOW, [(0, KEPT)])
    over_pairs(0, 4, 4, lambda p: window_back(3, p))
    back[1].wait_recv()
    fine_rows_back(2 * WINDOW, WINDOW, with_lon)
    over_pairs(0, 4, 4, lambda p: window_back(2, p))
    back[0].wait_recv()
    back[2].wait_recv()
    for part in out_c:
        part.start_second()
    fine_rows_back(0, 2 * WINDOW, whole)
    for h in range(2):
        r.grad_low[h] = r.grad_fine[:, h * 256 : (h + 1) * 256].astype(BF16)
    low_swap = swap(r.grad_low.at[1 - core], r.grad_low_other)

    def both_windows(p):
        window_back(0, p)
        window_back(1, p)

    pair_swaps = []
    for i in range(2):
        other, own = 2 * (1 - core) + i, 2 * core + i
        both_windows(other)
        r.grad_pair[other] = r.grad_packed[other].astype(BF16)
        pair_swaps.append(swap(r.grad_pair.at[other], r.grad_pair_other.at[i]))
        both_windows(own)
        r.grad_pair[own] = r.grad_packed[own].astype(BF16)
        if i == 0:
            mixed_swap.wait_recv()
            normed_swap.wait_recv()
            low_swap.wait_recv()
            both = jnp.concatenate([r.grad_low[core], r.grad_low_other[...]], axis=0)
            mixed_part = dot_tn(r.mixed[...].reshape(2 * CELLS, WIDE), both).astype(BF16)
            mixed_part = mixed_part.reshape(4, 4, HALF_ROWS, 256)
            for h in range(2):
                for g in range(4):
                    put_blocks(fine[h], g, 12, mixed_part[:, g, :, h * AUX : (h + 1) * AUX])
        pair_swaps[i].wait_recv()
        both = jnp.concatenate([r.grad_pair[own], r.grad_pair_other[i]], axis=0)
        grads = dot_tn(r.normed[...].reshape(2 * CELLS, WIDE), both)
        for t in range(3):
            r.mixed_rows[i, pl.ds(t, WIDE, stride=3), :] = grads[:, t * PAIR : (t + 1) * PAIR]
        for b in range(12):
            for g in range(4):
                rows = r.mixed_rows[i, pl.ds(b * 128 + g * 32, 32), :].astype(BF16)
                put_blocks(fine[i], g, b, rows[None])
        for part in fine[i]:
            part.start_first()
    grad_normed = jnp.zeros((CELLS, WIDE), F32)
    for t in range(3):
        grads = jnp.concatenate(
            [r.grad_pair[p, :, t * PAIR : (t + 1) * PAIR] for p in range(4)], axis=1
        )
        grad_normed += dot_nt(grads, r.v_w_qkv_fine[:, t * WIDE : (t + 1) * WIDE])
    normed, scale = norm_parts([r.cells[...]])
    (back_in,) = norm_parts_back(normed, scale, [grad_normed])
    grad_cells = (r.grad_fine[...] + back_in).astype(BF16)
    message = dot(spread(TAKE_WINDOWS_T, SLOTS, CELLS), grad_cells).astype(BF16)
    r.grad_send[...] = message[KEPT:]
    r.grad_recv[:KEPT] = message[:KEPT]
    grad = exchange(5, r.grad_send, r.grad_recv, PARTS, KEPT, up)
    for part in out_c:
        part.start_third()
    for part in merge:
        part.start_second()
    for part in fine[0] + fine[1]:
        part.start_second()
    for part in fine[0] + fine[1]:
        part.start_third()
    for part in merge:
        part.start_third()
    arrived(grad)
    r.grad_tokens[...] = dot(
        spread(SEND_ROWS_T, CELLS, SLOTS), r.grad_recv[...]
    ).astype(BF16)
    def finish_coarse():
        for part in out_c + merge:
            part.finish(r.total)
        copy = remote(
            r.total.at[1 - core], r.total_other, r.total_s.at[0], r.total_r.at[0], me.sibling()
        )
        copy.start()
        copy.wait()
        here, there = r.total[core], r.total_other[...]
        halves = [jnp.where(core == 0, here, there), jnp.where(core == 0, there, here)]
        for h in range(2):
            for c in range(4):
                r.grad_flat[pl.ds(4 * h + c, 32, stride=8), :] = halves[h][
                    :, c * AUX : (c + 1) * AUX
                ]

    def finish_fine():
        copies = []
        for i in range(2):
            for part in fine[i]:
                part.finish(r.fine_total.at[i])
            copies.append(
                remote(
                    r.fine_total.at[i, 1 - core], r.fine_total_other.at[i],
                    r.total_s.at[1 + i], r.total_r.at[1 + i], me.sibling(),
                )
            )
            copies[i].start()
        for i in range(2):
            copies[i].wait()
            here, there = r.fine_total[i, core], r.fine_total_other[i]
            halves = [jnp.where(core == 0, here, there), jnp.where(core == 0, there, here)]
            for h in range(2):
                for g in range(2):
                    r.grad_flat[pl.ds(g * 128 + 2 * h + i, 32, stride=4), :] = halves[h][
                        :, g * AUX : (g + 1) * AUX
                    ]

    when(me.lat >= 2, finish_coarse)
    when(me.lat < 2, finish_fine)
    for part in out_c + merge + fine[0] + fine[1]:
        part.drain()
    for copies in (tok, cot, top, out, back, grad, swaps):
        for copy in copies:
            copy.wait_send()


def per_device(n_lat, n_lon, tokens, cot_fine, cot_coarse, mask_ids, pad_flags,
               w_qkv_fine, w_out_fine, w_merge, w_qkv_coarse, w_out_coarse):
    given = dict(
        maps=jnp.asarray(index_maps()),
        tokens=tokens.reshape(CELLS, WIDE),
        cot_fine=cot_fine.reshape(CELLS, WIDE),
        cot_coarse=cot_coarse.reshape(cot_coarse.shape[1:]),
        w_qkv_fine=w_qkv_fine, w_out_fine=w_out_fine, w_merge=w_merge,
        w_qkv_coarse=w_qkv_coarse, w_out_coarse=w_out_coarse,
    )
    small = dict(
        mask_ids=mask_ids.reshape(ROWS, 1, COLS), pad_flags=pad_flags.reshape(ROWS, 1, COLS)
    )
    outs = dict(
        grad_tokens=((CELLS, WIDE), BF16),
        grad_flat=((256, AUX), F32),
    )
    scratch = {"v_" + name: (given[name].shape, given[name].dtype) for name in given}
    scratch.update(
        tok_send=((SLOTS - KEPT, WIDE + AUX), BF16),
        tok_recv=((SLOTS, WIDE + AUX), BF16),
        cot_send=((SLOTS - KEPT, WIDE), BF16),
        cot_recv=((SLOTS, WIDE), BF16),
        top_send=((SLOTS_C - KEPT_C, COARSE + AUX), BF16),
        top_recv=((SLOTS_C, COARSE + AUX), BF16),
        out_send=((SLOTS - KEPT, WIDE), BF16),
        out_recv=((SLOTS, WIDE), BF16),
        back_send=((SLOTS - KEPT, WIDE), BF16),
        back_recv=((SLOTS, WIDE), BF16),
        grad_send=((SLOTS - KEPT, WIDE), BF16),
        grad_recv=((SLOTS, WIDE), BF16),
        allowed=((4, 2 * WINDOW, WINDOW), F32),
        allowed_c=((1, 2 * WINDOW, WINDOW), F32),
        cells=((CELLS, WIDE), F32),
        fine_out=((CELLS, WIDE), BF16),
        normed=((2, CELLS, WIDE), BF16),
        packed=((4, CELLS, 3 * PAIR), F32),
        shares=((16, WINDOW, 2 * WINDOW), F32),
        attn=((4, CELLS, PAIR), F32),
        mixed=((2, CELLS, WIDE), BF16),
        top=((WINDOW, COARSE), F32),
        top_half=((2, 80, WIDE), BF16),
        top_other=((80, WIDE), BF16),
        grad_mixed_c=((8, WINDOW, PAIR), F32),
        merged=((4, WINDOW, WIDE), F32),
        normed_merge=((2, 80, 4 * WIDE), BF16),
        grad_merged=((4, WINDOW, WIDE), F32),
        coarse_in=((WINDOW, COARSE), F32),
        packed_c=((8, WINDOW, 3 * PAIR), F32),
        shares_c=((8, WINDOW, 2 * WINDOW), F32),
        attn_c=((8, WINDOW, PAIR), F32),
        mixed_c=((2, 80, COARSE), BF16),
        grad_packed_c=((8, WINDOW, 3 * PAIR), F32),
        grad_coarse=((2, 80, WIDE), BF16),
        grad_coarse_other=((80, WIDE), BF16),
        grad_fine=((CELLS, WIDE), F32),
        grad_low=((2, CELLS, 256), BF16),
        grad_low_other=((CELLS, 256), BF16),
        grad_packed=((4, CELLS, 3 * PAIR), F32),
        grad_pair=((4, CELLS, 3 * PAIR), BF16),
        grad_pair_other=((2, CELLS, 3 * PAIR), BF16),
        mixed_rows=((2, 3 * WIDE, AUX), F32),
        total=((2, HALF_ROWS, WIDE), F32),
        total_other=((HALF_ROWS, WIDE), F32),
        fine_total=((2, 2, HALF_ROWS, 256), F32),
        fine_total_other=((2, HALF_ROWS, 256), F32),
    )
    sems = dict(
        stage_sem=len(given), send_sem=18, recv_sem=18, swap_send=16, swap_recv=16,
        total_s=3, total_r=3,
    )
    for name, (_, lats, parts) in SEGMENTS.items():
        for axis, (_, cols) in parts.items():
            kept = kept_shape(lats, axis)
            block = (HALF_ROWS, cols)
            scratch["pa_" + name + axis] = ((lats, 4, 2) + block, BF16)
            scratch["ri_" + name + axis] = ((3,) + kept + block, BF16)
            scratch["la_" + name + axis] = (kept + block, BF16)
            scratch["fi_" + name + axis] = ((4,) + block, BF16)
            scratch["r2i_" + name + axis] = ((3, 2) + block, BF16)
            scratch["mid_" + name + axis] = ((2,) + block, BF16)
            sems["s1_" + name + axis] = sems["r1_" + name + axis] = 3
            sems["s2_" + name + axis] = sems["r2_" + name + axis] = 3
            sems["s3_" + name + axis], sems["r3_" + name + axis] = 2, 4
    names = (
        ["in_" + name for name in given] + list(small)
        + list(outs) + list(scratch) + list(sems)
    )

    def kernel(*refs):
        body(n_lat, n_lon, list(given), names, refs)

    vmem = pl.BlockSpec(memory_space=pltpu.VMEM)
    results = pl.pallas_call(
        kernel,
        out_shape=[jax.ShapeDtypeStruct(*s) for s in outs.values()],
        in_specs=[pl.BlockSpec(memory_space=pl.ANY)] * len(given) + [vmem, vmem],
        out_specs=[vmem] * len(outs),
        scratch_shapes=[pltpu.VMEM(*s) for s in scratch.values()]
        + [pltpu.SemaphoreType.DMA((n,)) for n in sems.values()],
        compiler_params=pltpu.CompilerParams(
            collective_id=0, has_side_effects=True, vmem_limit_bytes=60 * 2**20
        ),
        name="swin_backward",
    )(*[given[name] for name in given], *small.values())
    return results[0].reshape(tokens.shape), results[1].reshape(-1)


def solution(mesh):
    cells = P(None, "lat", "lon", None)
    ids = P(None, "lat", "lon")
    step = functools.partial(per_device, mesh.shape["lat"], mesh.shape["lon"])
    return jax.shard_map(
        step,
        mesh=mesh,
        in_specs=(cells, cells, cells, ids, ids) + (P(),) * 5,
        out_specs=(cells, P(("lat", "lon"))),
        check_vma=False,
    )
```

```python
import functools
import types

import jax
import jax.numpy as jnp
import numpy as np
from jax import lax
from jax.experimental import pallas as pl
from jax.experimental.pallas import tpu as pltpu
from jax.sharding import PartitionSpec as P

WIN_LAT = 6
WIN_LON = 12
ROWS = 12
COLS = 24
CELLS = ROWS * COLS
WINDOW = WIN_LAT * WIN_LON
WIDE = 512
COARSE = 1024
HEAD = 64
PAIR = 2 * HEAD
AUX = 128
MESH = pl.DeviceIdType.MESH
F32 = jnp.float32
BF16 = jnp.bfloat16

KEPT = 176
PARTS = ((176, 64), (240, 64), (304, 32))
SLOTS = 336
KEPT_C = 32
PARTS_C = ((32, 32), (64, 32), (96, 32))
SLOTS_C = 128


def slot_of(a, b, half_lat, half_lon, cols, offsets):
    if a >= half_lat and b >= half_lon:
        return (a - half_lat) * (cols - half_lon) + b - half_lon
    if b >= half_lon:
        return offsets[0] + a * (cols - half_lon) + b - half_lon
    if a >= half_lat:
        return offsets[1] + (a - half_lat) * half_lon + b
    return offsets[2] + a * half_lon + b


(
    SEND_ROWS, TAKE_WINDOWS, SEND_WINDOWS, TAKE_MERGE,
    SEND_ROWS_T, TAKE_WINDOWS_T, SEND_WINDOWS_T, TAKE_MERGE_T,
    SEND_COARSE, TAKE_COARSE, SEND_IDS, ROW_OF, COL_OF,
) = range(13)


def index_maps():
    fine = [off for off, _ in PARTS]
    coarse = [off for off, _ in PARTS_C]
    table = np.full((SLOTS, AUX), -1, np.int32)
    for a in range(ROWS):
        for b in range(COLS):
            cell = a * COLS + b
            here = slot_of(a, b, 3, 6, COLS, fine)
            came = slot_of((a + 3) % ROWS, (b + 6) % COLS, 3, 6, COLS, fine)
            window = (a // 6 * 2 + b // 12) * WINDOW + a % 6 * 12 + b % 12
            quarter = (a % 2 * 2 + b % 2) * WINDOW + a // 2 * 12 + b // 2
            for name, row, source in (
                (SEND_ROWS, here, cell),
                (TAKE_WINDOWS, window, came),
                (SEND_WINDOWS, here, window),
                (TAKE_MERGE, quarter, came),
            ):
                table[row, name] = source
                table[source, name + SEND_ROWS_T] = row
            table[cell, ROW_OF] = a
            table[cell, COL_OF] = b
    for i in range(6):
        for j in range(12):
            here = slot_of(i, j, 3, 6, 12, coarse)
            came = slot_of((i + 3) % 6, (j + 6) % 12, 3, 6, 12, coarse)
            table[here, SEND_COARSE] = i * 12 + j
            table[i * 12 + j, TAKE_COARSE] = came
            table[here, SEND_IDS] = 2 * i * COLS + 2 * j
    return table


def dot(a, b):
    return jnp.dot(a, b, preferred_element_type=F32)


def dot_nt(a, b):
    return lax.dot_general(a, b, (((1,), (1,)), ((), ())), preferred_element_type=F32)


def dot_tn(a, b):
    return lax.dot_general(a, b, (((0,), (0,)), ((), ())), preferred_element_type=F32)


def norm_parts(parts):
    size = sum(p.shape[-1] for p in parts)
    average = sum(jnp.sum(p, axis=-1, keepdims=True) for p in parts) * (1.0 / size)
    centred = [p - average for p in parts]
    spread = sum(jnp.sum(c * c, axis=-1, keepdims=True) for c in centred) * (1.0 / size)
    scale = lax.rsqrt(spread + 1e-05)
    return [c * scale for c in centred], scale


def norm_parts_back(normed, scale, grads):
    size = sum(p.shape[-1] for p in normed)
    flat = sum(jnp.sum(g, axis=-1, keepdims=True) for g in grads) * (1.0 / size)
    along = sum(
        jnp.sum(g * n, axis=-1, keepdims=True) for g, n in zip(grads, normed)
    ) * (1.0 / size)
    return [scale * (g - flat - n * along) for g, n in zip(grads, normed)]


def first_lanes():
    return lax.broadcasted_iota(jnp.int32, (WINDOW, PAIR), 1) < HEAD


def stacked(x, low):
    return jnp.concatenate([jnp.where(low, x, 0.0), jnp.where(low, 0.0, x)], axis=0)


def split_bf16(x):
    high = x.astype(BF16)
    return high, (x - high.astype(F32)).astype(BF16)


def allowed_of(ids):
    pick = (lax.broadcasted_iota(jnp.int32, (8, AUX), 1) == 0).astype(BF16)
    along = dot_nt(pick, ids.astype(BF16))[0:1]
    same = jnp.where(ids[:, 0:1] == along, 1.0, 0.0)
    return jnp.concatenate([same, same], axis=0)


def pair_forward(q, k, v, allowed, low):
    q_high, q_low = split_bf16(stacked(q * HEAD**-0.5, low))
    k_high, k_low = split_bf16(k)
    scores = dot_nt(
        jnp.concatenate([q_high, q_low], axis=1), jnp.concatenate([k_high, k_high], axis=1)
    ) + dot_nt(q_high, k_low)
    scores = jnp.where(allowed > 0.0, scores, -1e30)
    weights = jnp.exp(scores - jnp.max(scores, axis=-1, keepdims=True)).astype(BF16)
    result = dot(weights, jnp.concatenate([v.astype(BF16), jnp.ones_like(v, BF16)], axis=1))
    scale = 1.0 / result[:, PAIR:]
    result = result[:, :PAIR] * scale
    shares = weights.astype(F32) * scale[:, :WINDOW]
    return shares.T, jnp.where(low, result[:WINDOW], result[WINDOW:])


def pair_backward(q, k, v, shares, grad, low):
    grad2 = stacked(grad, low).astype(BF16)
    q2 = stacked(q, low).astype(BF16)
    grad_shares = dot_nt(v.astype(BF16), grad2)
    delta = jnp.sum(grad_shares * shares, axis=0, keepdims=True)
    grad_scores = (shares * (grad_shares - delta) * HEAD**-0.5).astype(BF16)
    grad_q = dot_tn(grad_scores, k.astype(BF16))
    grad_q = jnp.where(low, grad_q[:WINDOW], grad_q[WINDOW:])
    return grad_q, dot(grad_scores, q2), dot(shares.astype(BF16), grad2)


def attend(packed, shares, attn, allowed, w, p, pairs):
    rows = slice(w * WINDOW, (w + 1) * WINDOW)
    low = first_lanes()
    q, k, v = (packed[p, rows, t * PAIR : (t + 1) * PAIR] for t in range(3))
    part, result = pair_forward(q, k, v, allowed[w], low)
    shares[w * pairs + p] = part
    attn[p, rows] = result


def attend_back(packed, shares, grad, grad_packed, w, p, pairs):
    rows = slice(w * WINDOW, (w + 1) * WINDOW)
    low = first_lanes()
    q, k, v = (packed[p, rows, t * PAIR : (t + 1) * PAIR] for t in range(3))
    grads = pair_backward(q, k, v, shares[w * pairs + p], grad[p, rows], low)
    for t in range(3):
        grad_packed[p, rows, t * PAIR : (t + 1) * PAIR] = grads[t]


def over_pairs(first, pairs, step, unit):
    def some(n, carry):
        for i in range(step):
            unit(first + n * step + i)
        return carry

    lax.fori_loop(0, pairs // step, some, 0)


SEGMENTS = dict(
    out_c=(6, 2, dict(z=(0, 512), y=(512, 256), x=(768, 256))),
    merge=(2, 4, dict(z=(0, 384), y=(384, 384), x=(768, 256))),
    fine0=(0, 2, dict(z=(0, 256), y=(256, 128), x=(384, 128))),
    fine1=(0, 2, dict(z=(0, 256), y=(256, 128), x=(384, 128))),
)
HALF_ROWS = 32


class Place:
    def __init__(self, lat, lon):
        self.lat, self.y, self.x_high = lat, lat % 4, lat // 4
        self.z, self.x_low, self.core = lon // 4, lon // 2 % 2, lon % 2
        self.x = self.x_high * 2 + self.x_low

    def chip(self, x, y, z):
        return (x // 2 * 4 + y, z * 4 + x % 2 * 2 + self.core)

    def shifted(self, dx, dy, dz):
        return self.chip(
            lax.rem(self.x + dx, 4), lax.rem(self.y + dy, 4), lax.rem(self.z + dz, 4)
        )

    def sibling(self):
        return (self.lat, self.z * 4 + self.x_low * 2 + 1 - self.core)


def remote(src, dst, send_sem, recv_sem, peer):
    return pltpu.make_async_remote_copy(
        src_ref=src, dst_ref=dst, send_sem=send_sem, recv_sem=recv_sem,
        device_id=peer, device_id_type=MESH,
    )


class Part:
    def __init__(self, r, name, axis, me):
        self.first, self.lats, parts = SEGMENTS[name]
        self.left, self.cols = parts[axis]
        self.axis, self.me, self.all = axis, me, self.lats == 4
        (self.part, self.ring, self.last, self.final, self.send, self.recv, self.send2,
         self.recv2) = (
            getattr(r, what + name + axis)
            for what in ("pa_", "ri_", "la_", "fi_", "s1_", "r1_", "s2_", "r2_")
        )
        self.kept = kept_shape(self.lats, axis)
        self.ring2, self.mid, self.send3, self.recv3 = (
            getattr(r, what + name + axis) for what in ("r2i_", "mid_", "s3_", "r3_")
        )
        self.axis2 = {"z": "y", "y": "z", "x": "z"}[axis]
        self.axis3 = {"z": "x", "y": "x", "x": "y"}[axis]
        self.number3 = {"x": me.x, "y": me.y}[self.axis3]
        self.holds = True
        if not self.all and axis != "z":
            self.holds = self.among(me.y if axis == "y" else me.x)
        self.holds2 = self.holds
        if not self.all and axis == "z":
            self.holds2 = self.among(me.y)
        self.owns = jnp.logical_and(me.lat >= self.first, me.lat < self.first + self.lats)

    def among(self, index):
        return index // 2 == self.first // 4

    def source(self, to):
        if self.axis == "z":
            return self.part.at[:, to], True
        if self.axis == "x":
            if self.all:
                return self.part.at[pl.ds(to // 2 * 2, 2), :, to % 2], True
            return self.part.at[:, :, to % 2], self.among(to)
        if self.all:
            return self.part.at[lax.rem(to + 2, 4)], True
        return self.part.at[to % 2], self.among(to)

    def mine(self, i, j):
        me = self.me
        if self.axis == "z":
            return self.part[i, me.z, j]
        if self.axis == "x":
            return self.part[(me.x_high * 2 if self.all else 0) + i, j, me.x_low]
        return self.part[lax.rem(me.y + 2, 4) if self.all else me.y % 2, i, j]

    def firsts(self):
        me = self.me
        here = {"x": me.x, "y": me.y, "z": me.z}[self.axis]
        for d in range(1, 4):
            src, some = self.source(lax.rem(here + d, 4))
            shift = [d if self.axis == a else 0 for a in "xyz"]
            yield some, remote(
                src, self.ring.at[d - 1], self.send.at[d - 1], self.recv.at[d - 1],
                me.shifted(*shift),
            )

    def thirds(self):
        me = self.me
        for i in range(2):
            if self.axis3 == "x":
                to = ((1 - me.y // 2) if self.all else self.first // 4) * 2 + i
                peer = me.chip(to, me.y, me.z)
            else:
                to = 2 * ((1 - me.x_high) if self.all else self.first // 4) + i
                peer = me.chip(me.x, to, me.z)
            yield both(self.holds2, to != self.number3), remote(
                self.mid.at[i], self.final.at[self.number3], self.send3.at[i],
                self.recv3.at[self.number3], peer,
            )

    def seconds(self):
        me = self.me
        here = {"y": me.y, "z": me.z}[self.axis2]
        for d in range(1, 4):
            to = lax.rem(here + d, 4)
            going = self.holds
            src = {"z": lax.rem(to + 2, 4), "y": to, "x": (slice(None), to)}[self.axis]
            if self.axis == "z" and not self.all:
                src, going = to % 2, both(going, self.among(to))
            shift = [d if self.axis2 == a else 0 for a in "xyz"]
            yield going, remote(
                self.last.at[src], self.ring2.at[d - 1], self.send2.at[d - 1],
                self.recv2.at[d - 1], me.shifted(*shift),
            )

    def start_third(self):
        me = self.me

        def add():
            for _, copy in self.seconds():
                copy.wait_recv()
            for i in range(2):
                own = {
                    "z": (lax.rem(me.y + 2, 4) if self.all else me.y % 2, i),
                    "y": (me.z, i), "x": (i, me.z),
                }[self.axis]
                total = self.last[own].astype(F32)
                for d in range(3):
                    total += self.ring2[d, i].astype(F32)
                self.mid[i] = total.astype(BF16)

        when(self.holds2, add)
        for going, copy in self.thirds():
            when(going, copy.start)

    def start_first(self):
        for some, copy in self.firsts():
            when(some, copy.start)

    def start_second(self):
        def add():
            for _, copy in self.firsts():
                copy.wait_recv()
            for i in range(self.kept[0]):
                for j in range(self.kept[1]):
                    total = self.mine(i, j).astype(F32)
                    for d in range(3):
                        total += self.ring[d, i, j].astype(F32)
                    self.last[i, j] = total.astype(BF16)

        when(self.holds, add)
        for going, copy in self.seconds():
            when(going, copy.start)

    def finish(self, total):
        me = self.me

        def add():
            for n in range(4):
                copy = remote(
                    self.mid.at[0], self.final.at[n], self.send3.at[0], self.recv3.at[n],
                    me.sibling(),
                )
                when(self.number3 != n, copy.wait_recv)
            self.final[self.number3] = self.mid[me.x_low if self.axis3 == "x" else me.y % 2]
            for c in range(0, self.cols, AUX):
                value = self.final[0, :, c : c + AUX].astype(F32)
                for n in range(1, 4):
                    value += self.final[n, :, c : c + AUX].astype(F32)
                at = self.left + c
                half = total.shape[-1]
                total[at // half, :, at % half : at % half + AUX] = value

        when(self.owns, add)

    def drain(self):
        for some, copy in self.firsts():
            when(some, copy.wait_send)
        for going, copy in self.seconds():
            when(going, copy.wait_send)
        for going, copy in self.thirds():
            when(going, copy.wait_send)


def both(one, other):
    return other if one is True else one if other is True else jnp.logical_and(one, other)


def when(condition, step):
    if condition is True:
        step()
    else:
        pl.when(condition)(step)


def kept_shape(lats, axis):
    return {"z": (lats, 2), "x": (2, 4), "y": (4, 2)}[axis]


def put_blocks(parts, group, first, value):
    size = value.shape[-1]
    for part in parts:
        low = max(group * size, part.left)
        high = min((group + 1) * size, part.left + part.cols)
        if low < high:
            for b in range(value.shape[0]):
                n = first + b
                part.part[n // 8, n // 2 % 4, n % 2, :, low - part.left : high - part.left] = (
                    value[b, :, low - group * size : high - group * size]
                )


def eighty(x):
    return jnp.concatenate([x, jnp.zeros((80 - x.shape[0], x.shape[1]), x.dtype)], axis=0)


def body(n_lat, n_lon, given, names, refs):
    r = types.SimpleNamespace(**dict(zip(names, refs)))
    lat, lon = lax.axis_index("lat"), lax.axis_index("lon")
    lat_up, lat_down = lax.rem(lat + 1, n_lat), lax.rem(lat + n_lat - 1, n_lat)
    lon_up, lon_down = lax.rem(lon + 1, n_lon), lax.rem(lon + n_lon - 1, n_lon)
    down = ((lat_down, lon), (lat, lon_down), (lat_down, lon_down))
    up = ((lat_up, lon), (lat, lon_up), (lat_up, lon_up))

    staged = types.SimpleNamespace()
    for i, name in enumerate(given):
        copy = pltpu.make_async_copy(
            getattr(r, "in_" + name), getattr(r, "v_" + name), r.stage_sem.at[i]
        )
        setattr(staged, name, copy)
        copy.start()

    barrier = pltpu.get_barrier_semaphore()
    me = Place(lat, lon)
    core = me.core
    peers = [down[1], down[2], up[1], up[2]]
    for a in range(4):
        for b in range(4):
            peers += [me.shifted(a, b, 0)] if a or b else []
        peers += [me.shifted(0, 0, a)] if a else []
    for peer in peers:
        pl.semaphore_signal(barrier, inc=1, device_id=peer, device_id_type=MESH)

    sums = {
        name: [Part(r, name, axis, me) for axis in parts]
        for name, (_, _, parts) in SEGMENTS.items()
    }
    out_c, merge, *fine = sums.values()

    def exchange(turn, src, dst, parts, kept, peers, which=(0, 1, 2)):
        copies = []
        for i in which:
            off, size = parts[i]
            copies.append(
                remote(
                    src.at[pl.ds(off - kept, size)], dst.at[pl.ds(off, size)],
                    r.send_sem.at[3 * turn + i], r.recv_sem.at[3 * turn + i], peers[i],
                )
            )
            copies[-1].start()
        return copies

    def arrived(copies):
        for copy in copies:
            copy.wait_recv()

    swaps = []

    def swap(src, dst):
        n = len(swaps)
        swaps.append(remote(src, dst, r.swap_send.at[n], r.swap_recv.at[n], me.sibling()))
        swaps[-1].start()
        return swaps[-1]

    def one_hot(name, rows, cols, first=0, base=0):
        wanted = r.v_maps[first : first + rows, name : name + 1] - base
        place = lax.broadcasted_iota(jnp.int32, (rows, cols), 1)
        return jnp.where(place == wanted, 1.0, 0.0)

    def spread(name, rows, cols, first=0, base=0):
        return one_hot(name, rows, cols, first, base).astype(BF16)

    staged.maps.wait()
    staged.tokens.wait()
    send_rows = spread(SEND_ROWS, SLOTS, CELLS)
    mask = r.mask_ids[:, 0, :].astype(F32).astype(BF16)
    flags = r.pad_flags[:, 0, :].astype(F32).astype(BF16)
    row_of, col_of = spread(ROW_OF, CELLS, ROWS), one_hot(COL_OF, CELLS, COLS)
    ids = jnp.sum(dot(row_of, mask) * col_of, axis=-1, keepdims=True)
    flag_rows = jnp.sum(dot(row_of, flags) * col_of, axis=-1, keepdims=True)
    aux = jnp.where(
        lax.broadcasted_iota(jnp.int32, (CELLS, AUX), 1) == 0, ids, 0.0
    ).astype(BF16)
    message = dot(send_rows, r.v_tokens[...]).astype(BF16)
    r.tok_send[:, :WIDE] = message[KEPT:]
    r.tok_recv[:KEPT, :WIDE] = message[:KEPT]
    message = dot(send_rows, aux).astype(BF16)
    r.tok_send[:, WIDE:] = message[KEPT:]
    r.tok_recv[:KEPT, WIDE:] = message[:KEPT]
    pl.semaphore_wait(barrier, len(peers))
    tok = exchange(0, r.tok_send, r.tok_recv, PARTS, KEPT, down)
    staged.cot_fine.wait()
    flagged = (r.v_cot_fine[...].astype(F32) * flag_rows).astype(BF16)
    message = dot(send_rows, flagged).astype(BF16)
    r.cot_send[...] = message[KEPT:]
    r.cot_recv[:KEPT] = message[:KEPT]
    staged.cot_coarse.wait()
    message = jnp.zeros((SLOTS_C, COARSE), F32)
    for i in range(6):
        message += dot(spread(SEND_COARSE, SLOTS_C, 12, 0, 12 * i), r.v_cot_coarse[i])
    message = message.astype(BF16)
    r.top_send[:, :COARSE] = message[KEPT_C:]
    r.top_recv[:KEPT_C, :COARSE] = message[:KEPT_C]
    message = dot(spread(SEND_IDS, SLOTS_C, CELLS), aux).astype(BF16)
    r.top_send[:, COARSE:] = message[KEPT_C:]
    r.top_recv[:KEPT_C, COARSE:] = message[:KEPT_C]

    def taken(name, first, count, source, ranges, cols):
        return sum(
            dot(spread(name, count, size, first, off), source[off : off + size, cols])
            for off, size in ranges
        )

    def fine_rows(first, count, ranges):
        rows = slice(first, first + count)
        ids = taken(TAKE_WINDOWS, first, count, r.tok_recv, ranges, slice(WIDE, WIDE + AUX))
        for w in range(count // WINDOW):
            r.allowed[first // WINDOW + w] = allowed_of(ids[w * WINDOW : (w + 1) * WINDOW])
        r.cells[rows] = taken(
            TAKE_WINDOWS, first, count, r.tok_recv, ranges, slice(0, WIDE)
        )
        (normed,), _ = norm_parts([r.cells[rows]])
        normed = normed.astype(BF16)
        for t in range(3):
            packed = dot(normed, r.v_w_qkv_fine[:, t * WIDE : (t + 1) * WIDE])
            for p in range(4):
                r.packed[p, rows, t * PAIR : (t + 1) * PAIR] = packed[
                    :, p * PAIR : (p + 1) * PAIR
                ]

    def fine_attend(w, p):
        attend(r.packed, r.shares, r.attn, r.allowed, w, p, 4)

    def fine_result(first, count):
        rows = slice(first, first + count)
        mixed = jnp.concatenate([r.attn[p, rows] for p in range(4)], axis=1).astype(BF16)
        r.mixed[0, rows] = mixed
        fine_out = r.cells[rows] + dot(mixed, r.v_w_out_fine[...])
        r.fine_out[rows] = fine_out.astype(BF16)

    def fine_message(rows, slots):
        first, size = slots
        return dot(spread(SEND_WINDOWS, size, rows, first), r.fine_out[:rows]).astype(BF16)

    staged.w_qkv_fine.wait()
    whole = [(0, SLOTS)]
    with_lon = [(0, KEPT), PARTS[1]]
    fine_rows(0, WINDOW, [(0, KEPT)])
    over_pairs(0, 4, 4, lambda p: fine_attend(0, p))
    tok[1].wait_recv()
    fine_rows(WINDOW, WINDOW, with_lon)
    over_pairs(0, 4, 4, lambda p: fine_attend(1, p))
    staged.w_out_fine.wait()
    fine_result(0, 2 * WINDOW)
    for i in (0, 2):
        off, size = PARTS[i]
        r.out_send[off - KEPT : off - KEPT + size] = fine_message(2 * WINDOW, PARTS[i])
    out = exchange(3, r.out_send, r.out_recv, PARTS, KEPT, down, (0, 2))
    tok[0].wait_recv()
    tok[2].wait_recv()
    top = exchange(2, r.top_send, r.top_recv, PARTS_C, KEPT_C, down)
    fine_rows(2 * WINDOW, 2 * WINDOW, whole)
    over_pairs(0, 4, 4, lambda p: fine_attend(2, p))
    fine_result(2 * WINDOW, WINDOW)
    off, size = PARTS[1]
    r.out_send[off - KEPT : off - KEPT + size] = fine_message(3 * WINDOW, PARTS[1])
    out += exchange(3, r.out_send, r.out_recv, PARTS, KEPT, down, (1,))
    over_pairs(0, 4, 4, lambda p: fine_attend(3, p))
    fine_result(3 * WINDOW, WINDOW)
    r.out_recv[:KEPT] = fine_message(CELLS, (0, KEPT))

    (normed,), _ = norm_parts([r.cells[...]])
    r.normed[0] = normed.astype(BF16)
    normed_swap = swap(r.normed.at[0], r.normed.at[1])
    mixed_swap = swap(r.mixed.at[0], r.mixed.at[1])
    staged.w_merge.wait()
    arrived(out)
    cot = exchange(1, r.cot_send, r.cot_recv, PARTS, KEPT, down)
    for k in range(4):
        r.merged[k] = dot(spread(TAKE_MERGE, WINDOW, SLOTS, k * WINDOW), r.out_recv[...])
    normed, _ = norm_parts([r.merged[k] for k in range(4)])
    coarse_in = jnp.zeros((WINDOW, COARSE), F32)
    for k in range(4):
        part = eighty(normed[k]).astype(BF16)
        r.normed_merge[0, :, k * WIDE : (k + 1) * WIDE] = part
        coarse_in += dot(
            normed[k].astype(BF16), r.v_w_merge[k * WIDE : (k + 1) * WIDE]
        )
    merge_swap = swap(r.normed_merge.at[0], r.normed_merge.at[1])
    r.coarse_in[...] = coarse_in.astype(BF16).astype(F32)
    (normed,), _ = norm_parts([r.coarse_in[...]])
    normed = normed.astype(BF16)
    staged.w_qkv_coarse.wait()
    for t in range(6):
        packed = dot(normed, r.v_w_qkv_coarse[:, t * WIDE : (t + 1) * WIDE])
        for p in range(4):
            r.packed_c[t % 2 * 4 + p, :, t // 2 * PAIR : (t // 2 + 1) * PAIR] = packed[
                :, p * PAIR : (p + 1) * PAIR
            ]
    staged.w_out_coarse.wait()
    take_coarse = spread(TAKE_COARSE, WINDOW, SLOTS_C)
    arrived(top)
    r.allowed_c[0] = allowed_of(dot(take_coarse, r.top_recv[:, COARSE:]))
    r.top[...] = dot(take_coarse, r.top_recv[:, :COARSE])
    for h in range(2):
        r.top_half[h] = eighty(r.top[:, h * WIDE : (h + 1) * WIDE]).astype(BF16)
    top_swap = swap(r.top_half.at[1 - core], r.top_other)
    over_pairs(0, 8, 4, lambda p: attend(
        r.packed_c, r.shares_c, r.attn_c, r.allowed_c, 0, p, 8
    ))
    for p in range(8):
        r.mixed_c[0, :, p * PAIR : (p + 1) * PAIR] = eighty(r.attn_c[p]).astype(BF16)
    mixed_c_swap = swap(r.mixed_c.at[0], r.mixed_c.at[1])

    grad_mixed = dot_nt(r.top[...].astype(BF16), r.v_w_out_coarse[...])
    for p in range(8):
        r.grad_mixed_c[p] = grad_mixed[:, p * PAIR : (p + 1) * PAIR].astype(BF16).astype(F32)

    def coarse_back(p):
        attend_back(r.packed_c, r.shares_c, r.grad_mixed_c, r.grad_packed_c, 0, p, 8)

    over_pairs(0, 4, 4, coarse_back)
    mixed_c_swap.wait_recv()
    top_swap.wait_recv()
    both = jnp.concatenate([r.top_half[core], r.top_other[...]], axis=0)
    for t in range(2):
        mixed = r.mixed_c[:, :, t * WIDE : (t + 1) * WIDE].reshape(160, WIDE)
        part = dot_tn(mixed, both).astype(BF16).reshape(8, 2, HALF_ROWS, WIDE)
        for g in range(2):
            put_blocks(out_c, g, t * 8, part[:, g])
    for part in out_c:
        part.start_first()
    over_pairs(4, 4, 4, coarse_back)
    grad_normed = jnp.zeros((WINDOW, COARSE), F32)
    for t in range(6):
        grads = jnp.concatenate(
            [
                r.grad_packed_c[t % 2 * 4 + p, :, t // 2 * PAIR : (t // 2 + 1) * PAIR]
                for p in range(4)
            ],
            axis=1,
        ).astype(BF16)
        grad_normed += dot_nt(grads, r.v_w_qkv_coarse[:, t * WIDE : (t + 1) * WIDE])
    normed, scale = norm_parts([r.coarse_in[...]])
    (back,) = norm_parts_back(normed, scale, [grad_normed])
    grad_coarse = r.top[...] + back
    for h in range(2):
        r.grad_coarse[h] = eighty(grad_coarse[:, h * WIDE : (h + 1) * WIDE]).astype(BF16)
    grad_coarse = grad_coarse.astype(BF16)
    coarse_swap = swap(r.grad_coarse.at[1 - core], r.grad_coarse_other)
    for k in range(4):
        r.grad_merged[k] = dot_nt(grad_coarse, r.v_w_merge[k * WIDE : (k + 1) * WIDE])
    normed, scale = norm_parts([r.merged[k] for k in range(4)])
    back = norm_parts_back(normed, scale, [r.grad_merged[k] for k in range(4)])
    back = jnp.concatenate(back, axis=0).astype(BF16)
    message = dot(spread(TAKE_MERGE_T, SLOTS, CELLS), back).astype(BF16)
    r.back_send[...] = message[KEPT:]
    r.back_recv[:KEPT] = message[:KEPT]
    back = exchange(4, r.back_send, r.back_recv, PARTS, KEPT, up)

    merge_swap.wait_recv()
    coarse_swap.wait_recv()
    both = jnp.concatenate([r.grad_coarse[core], r.grad_coarse_other[...]], axis=0)
    for k in range(4):
        normed = r.normed_merge[:, :, k * WIDE : (k + 1) * WIDE].reshape(160, WIDE)
        part = dot_tn(normed, both).astype(BF16).reshape(8, 2, HALF_ROWS, WIDE)
        for g in range(2):
            put_blocks(merge, g, k * 8, part[:, g])
    for part in merge:
        part.start_first()

    arrived(cot)
    r.grad_fine[...] = dot(spread(TAKE_WINDOWS, CELLS, SLOTS), r.cot_recv[...])

    def fine_rows_back(first, count, ranges):
        rows = slice(first, first + count)
        r.grad_fine[rows] += taken(
            SEND_WINDOWS_T, first, count, r.back_recv, ranges, slice(0, WIDE)
        )
        low = r.grad_fine[rows].astype(BF16)
        grad_mixed = dot_nt(low, r.v_w_out_fine[...])
        for p in range(4):
            r.attn[p, rows] = grad_mixed[:, p * PAIR : (p + 1) * PAIR].astype(BF16).astype(F32)

    def window_back(w, p):
        attend_back(r.packed, r.shares, r.attn, r.grad_packed, w, p, 4)

    fine_rows_back(3 * WINDOW, WINDOW, [(0, KEPT)])
    over_pairs(0, 4, 4, lambda p: window_back(3, p))
    back[1].wait_recv()
    fine_rows_back(2 * WINDOW, WINDOW, with_lon)
    over_pairs(0, 4, 4, lambda p: window_back(2, p))
    back[0].wait_recv()
    back[2].wait_recv()
    fine_rows_back(0, 2 * WINDOW, whole)
    for h in range(2):
        r.grad_low[h] = r.grad_fine[:, h * 256 : (h + 1) * 256].astype(BF16)
    low_swap = swap(r.grad_low.at[1 - core], r.grad_low_other)

    def both_windows(p):
        window_back(0, p)
        window_back(1, p)

    pair_swaps = []
    for i in range(2):
        other, own = 2 * (1 - core) + i, 2 * core + i
        both_windows(other)
        r.grad_pair[other] = r.grad_packed[other].astype(BF16)
        pair_swaps.append(swap(r.grad_pair.at[other], r.grad_pair_other.at[i]))
        both_windows(own)
        r.grad_pair[own] = r.grad_packed[own].astype(BF16)
        if i == 0:
            mixed_swap.wait_recv()
            normed_swap.wait_recv()
            low_swap.wait_recv()
            both = jnp.concatenate([r.grad_low[core], r.grad_low_other[...]], axis=0)
            mixed_part = dot_tn(r.mixed[...].reshape(2 * CELLS, WIDE), both).astype(BF16)
            mixed_part = mixed_part.reshape(4, 4, HALF_ROWS, 256)
            for h in range(2):
                for g in range(4):
                    put_blocks(fine[h], g, 12, mixed_part[:, g, :, h * AUX : (h + 1) * AUX])
        pair_swaps[i].wait_recv()
        both = jnp.concatenate([r.grad_pair[own], r.grad_pair_other[i]], axis=0)
        grads = dot_tn(r.normed[...].reshape(2 * CELLS, WIDE), both)
        for t in range(3):
            r.mixed_rows[i, pl.ds(t, WIDE, stride=3), :] = grads[:, t * PAIR : (t + 1) * PAIR]
        for b in range(12):
            for g in range(4):
                rows = r.mixed_rows[i, pl.ds(b * 128 + g * 32, 32), :].astype(BF16)
                put_blocks(fine[i], g, b, rows[None])
        for part in fine[i]:
            part.start_first()
    grad_normed = jnp.zeros((CELLS, WIDE), F32)
    for t in range(3):
        grads = jnp.concatenate(
            [r.grad_pair[p, :, t * PAIR : (t + 1) * PAIR] for p in range(4)], axis=1
        )
        grad_normed += dot_nt(grads, r.v_w_qkv_fine[:, t * WIDE : (t + 1) * WIDE])
    normed, scale = norm_parts([r.cells[...]])
    (back_in,) = norm_parts_back(normed, scale, [grad_normed])
    grad_cells = (r.grad_fine[...] + back_in).astype(BF16)
    message = dot(spread(TAKE_WINDOWS_T, SLOTS, CELLS), grad_cells).astype(BF16)
    r.grad_send[...] = message[KEPT:]
    r.grad_recv[:KEPT] = message[:KEPT]
    grad = exchange(5, r.grad_send, r.grad_recv, PARTS, KEPT, up)
    for part in out_c:
        part.start_second()
    for part in merge:
        part.start_second()
    for part in fine[0] + fine[1]:
        part.start_second()
    for part in out_c:
        part.start_third()
    for part in fine[0] + fine[1]:
        part.start_third()
    for part in merge:
        part.start_third()
    arrived(grad)
    r.grad_tokens[...] = dot(
        spread(SEND_ROWS_T, CELLS, SLOTS), r.grad_recv[...]
    ).astype(BF16)
    def finish_coarse():
        for part in out_c + merge:
            part.finish(r.total)
        copy = remote(
            r.total.at[1 - core], r.total_other, r.total_s.at[0], r.total_r.at[0], me.sibling()
        )
        copy.start()
        copy.wait()
        here, there = r.total[core], r.total_other[...]
        halves = [jnp.where(core == 0, here, there), jnp.where(core == 0, there, here)]
        for h in range(2):
            for c in range(4):
                r.grad_flat[pl.ds(4 * h + c, 32, stride=8), :] = halves[h][
                    :, c * AUX : (c + 1) * AUX
                ]

    def finish_fine():
        copies = []
        for i in range(2):
            for part in fine[i]:
                part.finish(r.fine_total.at[i])
            copies.append(
                remote(
                    r.fine_total.at[i, 1 - core], r.fine_total_other.at[i],
                    r.total_s.at[1 + i], r.total_r.at[1 + i], me.sibling(),
                )
            )
            copies[i].start()
        for i in range(2):
            copies[i].wait()
            here, there = r.fine_total[i, core], r.fine_total_other[i]
            halves = [jnp.where(core == 0, here, there), jnp.where(core == 0, there, here)]
            for h in range(2):
                for g in range(2):
                    r.grad_flat[pl.ds(g * 128 + 2 * h + i, 32, stride=4), :] = halves[h][
                        :, g * AUX : (g + 1) * AUX
                    ]

    when(me.lat >= 2, finish_coarse)
    when(me.lat < 2, finish_fine)
    for part in out_c + merge + fine[0] + fine[1]:
        part.drain()
    for copies in (tok, cot, top, out, back, grad, swaps):
        for copy in copies:
            copy.wait_send()


def per_device(n_lat, n_lon, tokens, cot_fine, cot_coarse, mask_ids, pad_flags,
               w_qkv_fine, w_out_fine, w_merge, w_qkv_coarse, w_out_coarse):
    given = dict(
        maps=jnp.asarray(index_maps()),
        tokens=tokens.reshape(CELLS, WIDE),
        cot_fine=cot_fine.reshape(CELLS, WIDE),
        cot_coarse=cot_coarse.reshape(cot_coarse.shape[1:]),
        w_qkv_fine=w_qkv_fine, w_out_fine=w_out_fine, w_merge=w_merge,
        w_qkv_coarse=w_qkv_coarse, w_out_coarse=w_out_coarse,
    )
    small = dict(
        mask_ids=mask_ids.reshape(ROWS, 1, COLS), pad_flags=pad_flags.reshape(ROWS, 1, COLS)
    )
    outs = dict(
        grad_tokens=((CELLS, WIDE), BF16),
        grad_flat=((256, AUX), F32),
    )
    scratch = {"v_" + name: (given[name].shape, given[name].dtype) for name in given}
    scratch.update(
        tok_send=((SLOTS - KEPT, WIDE + AUX), BF16),
        tok_recv=((SLOTS, WIDE + AUX), BF16),
        cot_send=((SLOTS - KEPT, WIDE), BF16),
        cot_recv=((SLOTS, WIDE), BF16),
        top_send=((SLOTS_C - KEPT_C, COARSE + AUX), BF16),
        top_recv=((SLOTS_C, COARSE + AUX), BF16),
        out_send=((SLOTS - KEPT, WIDE), BF16),
        out_recv=((SLOTS, WIDE), BF16),
        back_send=((SLOTS - KEPT, WIDE), BF16),
        back_recv=((SLOTS, WIDE), BF16),
        grad_send=((SLOTS - KEPT, WIDE), BF16),
        grad_recv=((SLOTS, WIDE), BF16),
        allowed=((4, 2 * WINDOW, WINDOW), F32),
        allowed_c=((1, 2 * WINDOW, WINDOW), F32),
        cells=((CELLS, WIDE), F32),
        fine_out=((CELLS, WIDE), BF16),
        normed=((2, CELLS, WIDE), BF16),
        packed=((4, CELLS, 3 * PAIR), F32),
        shares=((16, WINDOW, 2 * WINDOW), F32),
        attn=((4, CELLS, PAIR), F32),
        mixed=((2, CELLS, WIDE), BF16),
        top=((WINDOW, COARSE), F32),
        top_half=((2, 80, WIDE), BF16),
        top_other=((80, WIDE), BF16),
        grad_mixed_c=((8, WINDOW, PAIR), F32),
        merged=((4, WINDOW, WIDE), F32),
        normed_merge=((2, 80, 4 * WIDE), BF16),
        grad_merged=((4, WINDOW, WIDE), F32),
        coarse_in=((WINDOW, COARSE), F32),
        packed_c=((8, WINDOW, 3 * PAIR), F32),
        shares_c=((8, WINDOW, 2 * WINDOW), F32),
        attn_c=((8, WINDOW, PAIR), F32),
        mixed_c=((2, 80, COARSE), BF16),
        grad_packed_c=((8, WINDOW, 3 * PAIR), F32),
        grad_coarse=((2, 80, WIDE), BF16),
        grad_coarse_other=((80, WIDE), BF16),
        grad_fine=((CELLS, WIDE), F32),
        grad_low=((2, CELLS, 256), BF16),
        grad_low_other=((CELLS, 256), BF16),
        grad_packed=((4, CELLS, 3 * PAIR), F32),
        grad_pair=((4, CELLS, 3 * PAIR), BF16),
        grad_pair_other=((2, CELLS, 3 * PAIR), BF16),
        mixed_rows=((2, 3 * WIDE, AUX), F32),
        total=((2, HALF_ROWS, WIDE), F32),
        total_other=((HALF_ROWS, WIDE), F32),
        fine_total=((2, 2, HALF_ROWS, 256), F32),
        fine_total_other=((2, HALF_ROWS, 256), F32),
    )
    sems = dict(
        stage_sem=len(given), send_sem=18, recv_sem=18, swap_send=16, swap_recv=16,
        total_s=3, total_r=3,
    )
    for name, (_, lats, parts) in SEGMENTS.items():
        for axis, (_, cols) in parts.items():
            kept = kept_shape(lats, axis)
            block = (HALF_ROWS, cols)
            scratch["pa_" + name + axis] = ((lats, 4, 2) + block, BF16)
            scratch["ri_" + name + axis] = ((3,) + kept + block, BF16)
            scratch["la_" + name + axis] = (kept + block, BF16)
            scratch["fi_" + name + axis] = ((4,) + block, BF16)
            scratch["r2i_" + name + axis] = ((3, 2) + block, BF16)
            scratch["mid_" + name + axis] = ((2,) + block, BF16)
            sems["s1_" + name + axis] = sems["r1_" + name + axis] = 3
            sems["s2_" + name + axis] = sems["r2_" + name + axis] = 3
            sems["s3_" + name + axis], sems["r3_" + name + axis] = 2, 4
    names = (
        ["in_" + name for name in given] + list(small)
        + list(outs) + list(scratch) + list(sems)
    )

    def kernel(*refs):
        body(n_lat, n_lon, list(given), names, refs)

    vmem = pl.BlockSpec(memory_space=pltpu.VMEM)
    results = pl.pallas_call(
        kernel,
        out_shape=[jax.ShapeDtypeStruct(*s) for s in outs.values()],
        in_specs=[pl.BlockSpec(memory_space=pl.ANY)] * len(given) + [vmem, vmem],
        out_specs=[vmem] * len(outs),
        scratch_shapes=[pltpu.VMEM(*s) for s in scratch.values()]
        + [pltpu.SemaphoreType.DMA((n,)) for n in sems.values()],
        compiler_params=pltpu.CompilerParams(
            collective_id=0, has_side_effects=True, vmem_limit_bytes=60 * 2**20
        ),
        name="swin_backward",
    )(*[given[name] for name in given], *small.values())
    return results[0].reshape(tokens.shape), results[1].reshape(-1)


def solution(mesh):
    cells = P(None, "lat", "lon", None)
    ids = P(None, "lat", "lon")
    step = functools.partial(per_device, mesh.shape["lat"], mesh.shape["lon"])
    return jax.shard_map(
        step,
        mesh=mesh,
        in_specs=(cells, cells, cells, ids, ids) + (P(),) * 5,
        out_specs=(cells, P(("lat", "lon"))),
        check_vma=False,
    )
```
